32 devices in a mesh: groups: 2 (over x), fsdp: 16 (over z, y, core).
Axes of the slice: x: 2, y: 2, z: 4, core: 2. Of those that a mesh axis runs over, the one named last changes fastest.
Arguments:
- activations: bfloat16 [4096, 8192], P(('groups', 'fsdp')), parts along dimension 0, may hold values from -6 to 6
- grad_out: bfloat16 [4096, 1024], P(('groups', 'fsdp')), parts along dimension 0, may hold values from -1.5 to 1.5
- token_tenant: int32 [4096], P(('groups', 'fsdp')), parts along dimension 0, may hold values from -1 to 15, as said below
- segment_offsets: int32 [34], P('groups'), parts along dimension 0, may hold values from 0 to 2048, as said below
- value_weight: bfloat16 [8192, 1024], P('fsdp'), may hold values from -0.0625 to 0.0625
- down_weight_pool: bfloat16 [16, 16, 8192], P('fsdp'), may hold values from -0.0625 to 0.0625
- up_weight_pool: bfloat16 [16, 16, 1024], P('fsdp'), may hold values from -0.359375 to 0.359375
- page_table: int32 [16], replicated, may hold values from 0 to 15, each once
Outputs:
- adapted_value_output: bfloat16 [4096, 1024], P(('groups', 'fsdp')), parts along dimension 0
- input_gradient: bfloat16 [4096, 8192], P(('groups', 'fsdp')), parts along dimension 0
- down_pool_gradient: float32 [32, 16, 8192], P(('groups', 'fsdp')), parts along dimension 0
- up_pool_gradient: float32 [32, 16, 1024], P(('groups', 'fsdp')), parts along dimension 0
The draws below stay inside these ranges and needn't reach their ends.
There are 2 independent parts, one for each index of `groups`. The reference program is written for one: setup_inputs(seed, part) draws one part's arguments, and reference() takes and returns one part's arrays. A program takes and returns all parts, laid end to end along the dimension named above; an argument that names none is the same for every part. Nothing has to cross between parts.
Inputs may be any that keep to these rules, and one draw needn't show every extreme that they name: `token_tenant`: rows come in aligned blocks of 128 rows; all live rows of a block belong to one tenant and the first row of every block is live. Tenant ids never fall from block to block. Padding rows (-1) stand only at the end of the last block of a tenant's segment. A tenant's segment may span several devices; some tenants have no rows. `segment_offsets`: Multiples of 128, never falling, the first 0 and the last 2048; tenant t's blocks are rows segment_offsets[t] to segment_offsets[t + 1] - 1, in agreement with token_tenant. `page_table`: each slot holds exactly one tenant's page; slot s lies on device s of fsdp.
All inputs are finite; a program needn't handle non-finite values.
Results may differ from the reference program's by a relative error of at most 0.0031.
Values may be sent and summed in bfloat16 or wider, within the bound.
A program may use at most 128 MiB of HBM per device.

```python
import jax
import jax.numpy as jnp

D = 8192
DO = 1024
R = 16
BLOCK = 128
TENANTS = 16
TOKENS = 2048
BLOCKS = 16


def block_tenants(key):
    hot_key, pick_key, cold_key, coin_key = jax.random.split(key, 4)
    hot_ids = jax.random.randint(hot_key, (8,), 0, TENANTS)
    hot_pick = jax.random.randint(pick_key, (BLOCKS,), 0, 8)
    cold_ids = jax.random.randint(cold_key, (BLOCKS,), 0, TENANTS)
    coin_flip = jax.random.randint(coin_key, (BLOCKS,), 0, 3)
    return jnp.sort(jnp.where(coin_flip == 0, hot_ids[hot_pick], cold_ids)).astype(jnp.int32)


def draw_token_tenant(key, part):
    owners = block_tenants(key)
    key = jax.random.fold_in(key, 7)
    is_final = jnp.concatenate([owners[1:] != owners[:-1], jnp.array([True])])
    filled = jax.random.randint(key, (BLOCKS,), 1, BLOCK + 1)
    row_count = jnp.where(is_final, filled, BLOCK)
    row_place = jnp.arange(BLOCK, dtype=jnp.int32)[None, :]
    tenant_ids = jnp.where(row_place < row_count[:, None], owners[:, None], -1)
    return tenant_ids.reshape(TOKENS).astype(jnp.int32)


def draw_segment_offsets(key, part):
    owners = block_tenants(key)
    bounds = jnp.arange(TENANTS + 1, dtype=jnp.int32)
    below = jnp.sum((owners[None, :] < bounds[:, None]).astype(jnp.int32), axis=1)
    return (below * BLOCK).astype(jnp.int32)


def block_scale(rng, shape, pieces, smallest, largest):
    gain = 1.0
    for dim, blocks in pieces:
        heights = jax.random.uniform(jax.random.fold_in(jax.random.fold_in(rng, 6), dim), (blocks,), jnp.float32, smallest / len(pieces), largest / len(pieces))
        gain = gain * jnp.repeat(jnp.exp(heights), shape[dim] // blocks).reshape((-1,) + (1,) * (len(shape) - 1 - dim))
    return gain


def centred(stream_key, shape, spread, reach, shards=(), kind=jnp.bfloat16):
    drawn = spread * jax.random.normal(stream_key, shape, jnp.float32)
    if shards:
        drawn = drawn * block_scale(stream_key, shape, shards, -0.22, 0.18)
    return jnp.clip(drawn, -reach, reach).astype(kind)


def setup_inputs(seed: int = 0, part: int = 0) -> dict:
    streams_of = jax.random.split(jax.random.key(seed), 9)
    part_splits = jax.random.split(jax.random.fold_in(streams_of[8], part), 9)
    activations = centred(part_splits[0], (TOKENS, D), 1.0, 6.0, ((0, 16),))
    grad_out = centred(part_splits[1], (TOKENS, DO), 0.25, 1.5, ((0, 16),))
    token_tenant = draw_token_tenant(jax.random.fold_in(jax.random.fold_in(streams_of[8], part), 71), part)
    segment_offsets = draw_segment_offsets(jax.random.fold_in(jax.random.fold_in(streams_of[8], part), 71), part)
    value_weight = centred(streams_of[4], (D, DO), D ** -0.5, 0.0625, ((0, 16),))
    down_weight_pool = centred(streams_of[5], (TENANTS, R, D), D ** -0.5, 0.0625, ((0, 16),))
    up_weight_pool = centred(streams_of[6], (TENANTS, R, DO), 0.06, 0.359375, ((0, 16),))
    page_table = jax.random.permutation(streams_of[7], TENANTS).astype(jnp.int32)
    return {"activations": activations, "grad_out": grad_out, "token_tenant": token_tenant, "segment_offsets": segment_offsets, "value_weight": value_weight, "down_weight_pool": down_weight_pool, "up_weight_pool": up_weight_pool, "page_table": page_table}


adapter_scale_factor = 2.0


def reference(activations, grad_out, token_tenant, segment_offsets, value_weight, down_weight_pool, up_weight_pool, page_table):
    block_first = jnp.arange(BLOCKS, dtype=jnp.int32) * BLOCK
    block_tenant = jnp.sum((segment_offsets[1:][None, :] <= block_first[:, None]).astype(jnp.int32), axis=1).astype(jnp.int32)
    block_slot = page_table[block_tenant].astype(jnp.int32)
    active_token_rows = (token_tenant >= 0)
    masked_grad = grad_out * active_token_rows.astype(jnp.bfloat16)[:, None]
    down_pages = down_weight_pool[block_slot].astype(jnp.float32)
    up_pages = up_weight_pool[block_slot].astype(jnp.float32)
    input_blocks = activations.reshape(BLOCKS, BLOCK, D).astype(jnp.float32)
    gradient_blocks = masked_grad.reshape(BLOCKS, BLOCK, DO).astype(jnp.float32)
    reduced_rank_rows = jnp.einsum("bnd,brd->bnr", input_blocks, down_pages).astype(jnp.bfloat16)
    expanded_rows = jnp.einsum("bnr,bro->bno", reduced_rank_rows.astype(jnp.float32), up_pages).reshape(TOKENS, DO)
    base_output_rows = jnp.dot(activations, value_weight, preferred_element_type=jnp.float32)
    adapted_value_output = ((base_output_rows + adapter_scale_factor * expanded_rows) * active_token_rows.astype(jnp.float32)[:, None]).astype(jnp.bfloat16)
    pulled_rows = jnp.einsum("bno,bro->bnr", gradient_blocks, up_pages).astype(jnp.bfloat16)
    scattered_gradient = jnp.einsum("bnr,brd->bnd", pulled_rows.astype(jnp.float32), down_pages).reshape(TOKENS, D)
    base_gradient_input = jnp.dot(masked_grad, value_weight.T, preferred_element_type=jnp.float32)
    input_gradient = (base_gradient_input + adapter_scale_factor * scattered_gradient).astype(jnp.bfloat16)
    down_weight_terms = adapter_scale_factor * jnp.einsum("kpz,kpj->kzj", pulled_rows.astype(jnp.float32), input_blocks)
    up_weight_terms = adapter_scale_factor * jnp.einsum("yig,yiw->ygw", reduced_rank_rows.astype(jnp.float32), gradient_blocks)
    down_pool_gradient = jnp.zeros((TENANTS, R, D), jnp.float32).at[block_slot].add(down_weight_terms)
    up_pool_gradient = jnp.zeros((TENANTS, R, DO), jnp.float32).at[block_slot].add(up_weight_terms)
    return adapted_value_output, input_gradient, down_pool_gradient, up_pool_gradient
```

```python
import functools

import jax
import jax.numpy as jnp
from jax import lax
from jax.experimental import pallas as pl
from jax.experimental.pallas import tpu as pltpu
from jax.sharding import PartitionSpec as P

BLOCK = 128


adapter_scale_factor = 2.0


def on_device(
    activations,
    grad_out,
    token_tenant,
    segment_offsets,
    value_weight,
    down_weight_pool,
    up_weight_pool,
    page_table,
):
    devices = lax.axis_size("fsdp")
    tok_rows, hidden_model_width = activations.shape
    output_width = grad_out.shape[1]
    local_slot_count = down_weight_pool.shape[0]
    adapter_rank_size = down_weight_pool.shape[1]
    tenants = page_table.shape[0]
    local_block_count = tok_rows // BLOCK
    blocks_all = local_block_count * devices
    active_token_rows = token_tenant >= 0
    masked_grad = grad_out * active_token_rows.astype(jnp.bfloat16)[:, None]
    contract_last = (((1,), (1,)), ((), ()))
    full_weight = lax.all_gather(value_weight, "fsdp", axis=0, tiled=True)
    base_output_rows = jnp.dot(activations, full_weight, preferred_element_type=jnp.float32)
    base_gradient_input = lax.dot_general(
        masked_grad, full_weight, contract_last, preferred_element_type=jnp.float32
    )
    flattened_down_weight = down_weight_pool.reshape(
        local_slot_count, adapter_rank_size * hidden_model_width
    )
    flattened_up_weight = up_weight_pool.reshape(local_slot_count, adapter_rank_size * output_width)
    held_down, held_up = (
        lax.all_to_all(flattened_down_weight, "fsdp", split_axis=1, concat_axis=0, tiled=True),
        lax.all_to_all(flattened_up_weight, "fsdp", split_axis=1, concat_axis=0, tiled=True),
    )
    share_down = held_down.shape[1]
    share_up = held_up.shape[1]
    block_first = lax.iota(jnp.int32, blocks_all) * BLOCK
    block_tenant = jnp.sum(
        (segment_offsets[1:][None, :] <= block_first[:, None]).astype(jnp.int32), axis=1
    )
    tenant_match = block_tenant[:, None] == lax.iota(jnp.int32, tenants)[None, :]
    block_slot = jnp.sum(jnp.where(tenant_match, page_table[None, :], 0), axis=1)
    send_down = jnp.take(held_down, block_slot, axis=0).reshape(
        devices, local_block_count, share_down
    )
    send_up = jnp.take(held_up, block_slot, axis=0).reshape(devices, local_block_count, share_up)
    fetched_down_weight, fetched_up_weight = (
        lax.all_to_all(send_down, "fsdp", split_axis=0, concat_axis=2, tiled=True),
        lax.all_to_all(send_up, "fsdp", split_axis=0, concat_axis=2, tiled=True),
    )
    down_weight_block = fetched_down_weight.reshape(
        local_block_count, adapter_rank_size, hidden_model_width
    )
    up_weight_block = fetched_up_weight.reshape(local_block_count, adapter_rank_size, output_width)
    input_blocks = activations.reshape(local_block_count, BLOCK, hidden_model_width)
    gradient_blocks = masked_grad.reshape(local_block_count, BLOCK, output_width)
    reduced_rank_rows = jnp.einsum(
        "bnd,brd->bnr", input_blocks, down_weight_block, preferred_element_type=jnp.float32
    ).astype(jnp.bfloat16)
    expanded_rows = jnp.einsum(
        "bnr,bro->bno", reduced_rank_rows, up_weight_block, preferred_element_type=jnp.float32
    ).reshape(tok_rows, output_width)
    pulled_rows = jnp.einsum(
        "bno,bro->bnr", gradient_blocks, up_weight_block, preferred_element_type=jnp.float32
    ).astype(jnp.bfloat16)
    scattered_gradient = jnp.einsum(
        "bnr,brd->bnd", pulled_rows, down_weight_block, preferred_element_type=jnp.float32
    ).reshape(tok_rows, hidden_model_width)
    adapted_value_output = (
        (base_output_rows + adapter_scale_factor * expanded_rows)
        * active_token_rows.astype(jnp.float32)[:, None]
    ).astype(jnp.bfloat16)
    input_gradient = (base_gradient_input + adapter_scale_factor * scattered_gradient).astype(
        jnp.bfloat16
    )
    down_weight_terms = adapter_scale_factor * jnp.einsum(
        "kpz,kpj->kzj", pulled_rows, input_blocks, preferred_element_type=jnp.float32
    )
    up_weight_terms = adapter_scale_factor * jnp.einsum(
        "yig,yiw->ygw", reduced_rank_rows, gradient_blocks, preferred_element_type=jnp.float32
    )
    ret_down = down_weight_terms.reshape(local_block_count, devices, share_down)
    ret_up = up_weight_terms.reshape(local_block_count, devices, share_up)
    back_down, back_up = (
        lax.all_to_all(ret_down, "fsdp", split_axis=1, concat_axis=0, tiled=True),
        lax.all_to_all(ret_up, "fsdp", split_axis=1, concat_axis=0, tiled=True),
    )
    recv_down = back_down.reshape(blocks_all, share_down)
    recv_up = back_up.reshape(blocks_all, share_up)
    slot_match = (block_slot[None, :] == lax.iota(jnp.int32, tenants)[:, None]).astype(jnp.float32)
    sum_down = jnp.dot(
        slot_match, recv_down, precision=lax.Precision.HIGHEST, preferred_element_type=jnp.float32
    )
    sum_up = jnp.dot(
        slot_match, recv_up, precision=lax.Precision.HIGHEST, preferred_element_type=jnp.float32
    )
    resident_down_weight, resident_up_weight = (
        lax.all_to_all(sum_down, "fsdp", split_axis=0, concat_axis=1, tiled=True),
        lax.all_to_all(sum_up, "fsdp", split_axis=0, concat_axis=1, tiled=True),
    )
    down_pool_gradient = resident_down_weight.reshape(
        local_slot_count, adapter_rank_size, hidden_model_width
    )
    up_pool_gradient = resident_up_weight.reshape(local_slot_count, adapter_rank_size, output_width)
    return (adapted_value_output, input_gradient, down_pool_gradient, up_pool_gradient)


LAST = (((1,), (1,)), ((), ()))
FIRST = (((0,), (0,)), ((), ()))
LANES = 128


def remote(src, dst, send, recv, where):
    return pltpu.make_async_remote_copy(
        src_ref=src,
        dst_ref=dst,
        send_sem=send,
        recv_sem=recv,
        device_id=where,
        device_id_type=pl.DeviceIdType.MESH,
    )


def fused_kernel(
    n,
    acts,
    grad,
    tenant,
    offsets,
    table,
    w_hbm,
    down,
    up,
    out,
    ig,
    down_grad,
    up_grad,
    w_all,
    mg,
    total,
    share_out,
    share_in0,
    share_in1,
    share_in2,
    share_in3,
    slots,
    pulled2,
    live_col,
    local_sem,
    ring_send,
    ring_recv,
    x_send,
    x_recv,
    core_send,
    core_recv,
    corex_send,
    corex_recv,
    own_send,
    own_recv,
    share_send,
    share_recv,
):
    share_in = (share_in0, share_in1, share_in2, share_in3)
    x = lax.axis_index("groups")
    f = lax.axis_index("fsdp")
    m = n // 2
    half = m // 2
    chip, core = lax.div(f, 2), lax.rem(f, 2)
    z, y = lax.div(chip, 2), lax.rem(chip, 2)
    p = z + y * (m - 1 - 2 * z)
    width = down.shape[2] // n
    out_width = up.shape[2]
    ups = out_width // LANES
    rows = w_all.shape[1]
    cut = ((rows * 176) // 512) // 16 * 16
    length = rows - cut
    first = (length // 2 + 15) // 16 * 16

    def chip_at(position):
        q = lax.rem(position + 2 * m, m)
        y_q = lax.div(q, half)
        return 2 * (q + y_q * (m - 1 - 2 * q)) + y_q

    def at(shard, start, size):
        return w_all.at[shard, pl.ds(pl.multiple_of(start, 16), size), :]

    right = {"fsdp": 2 * chip_at(p + 1) + core}
    left = {"fsdp": 2 * chip_at(p - 1) + core}
    sibling = {"fsdp": 2 * chip + 1 - core}
    across = {"groups": 1 - x}
    ring_start = x * cut
    mine_start = x * length
    other_start = (1 - x) * length

    barrier = pltpu.get_barrier_semaphore()

    @pl.loop(1, n)
    def _(d):
        pl.semaphore_signal(
            barrier,
            inc=1,
            device_id={"fsdp": lax.rem(f + d, n)},
            device_id_type=pl.DeviceIdType.MESH,
        )

    pl.semaphore_signal(barrier, inc=1, device_id=across, device_id_type=pl.DeviceIdType.MESH)
    load = pltpu.make_async_copy(w_hbm, w_all.at[f], local_sem)
    load.start()
    for j in range(n):
        share_out[0, j, :, :width] = down[0, :, j * width : (j + 1) * width]
        k = j % ups
        share_out[0, j, :, width:] = up[0, :, k * LANES : (k + 1) * LANES]
    pl.semaphore_wait(barrier, n)

    def share_copy(phase, j, slot):
        return remote(
            share_out.at[phase, j],
            share_in[phase].at[slot],
            share_send.at[phase, j],
            share_recv.at[phase, slot],
            {"fsdp": j},
        )

    def share_start(phase):
        @pl.loop(1, n)
        def _(d):
            j = lax.rem(f + d, n)
            share_copy(phase, j, f).start()

        share_in[phase][f] = share_out[phase, f]

    def share_wait(phase):
        @pl.loop(1, n)
        def _(d):
            j = lax.rem(f + d, n)
            share_copy(phase, j, j).wait_recv()

    sends = []

    def go(copy):
        copy.start()
        sends.append(copy)

    def ring_copy(way, s, shard):
        if s < half:
            start, size = ring_start, length
        elif way == 0:
            start, size = ring_start, first
        else:
            start, size = ring_start + first, length - first
        part = at(shard, start, size)
        return remote(
            part,
            part,
            ring_send.at[way, s - 1],
            ring_recv.at[way, s - 1],
            (right, left)[way],
        )

    def x_copy(way, s, shard, start):
        part = at(shard, start, cut)
        return remote(part, part, x_send.at[way, s - 1], x_recv.at[way, s - 1], across)

    def core_copy(way, s, shard):
        part = at(shard, ring_start, length)
        return remote(part, part, core_send.at[way, s - 1], core_recv.at[way, s - 1], sibling)

    def corex_copy(way, s, shard):
        part = at(shard, other_start, cut)
        return remote(part, part, corex_send.at[way, s - 1], corex_recv.at[way, s - 1], sibling)

    def shard_of(way, s, c):
        return 2 * chip_at(p - s if way == 0 else p + s) + c

    def pass_on(s):
        for way in range(2):
            shard = shard_of(way, s, core)
            ring_copy(way, s, shard).wait_recv()
            if s < half:
                go(ring_copy(way, s + 1, shard))
                go(x_copy(way, s, shard, mine_start))
                go(core_copy(way, s, shard))
        if s == half:
            shard = shard_of(0, s, core)
            go(x_copy(0, s, shard, mine_start))
            go(core_copy(0, s, shard))

    def finish(s):
        ways = 2 if s < half else 1
        for way in range(ways):
            shard = shard_of(way, s, core)
            x_copy(way, s, shard, other_start).wait_recv()
            go(corex_copy(way, s, shard))
        for way in range(ways):
            shard = shard_of(way, s, 1 - core)
            core_copy(way, s, shard).wait_recv()
            corex_copy(way, s, shard).wait_recv()

    def consume(shard):
        columns = pl.ds(pl.multiple_of(shard * width, LANES), width)
        w = w_all[shard]
        total[...] += jnp.dot(acts[:, columns], w, preferred_element_type=jnp.float32)
        back = lax.dot_general(mg[...], w, LAST, preferred_element_type=jnp.float32)
        back += jnp.dot(
            pulled2[...], share_in1[shard, :, :width], preferred_element_type=jnp.float32
        )
        ig[:, columns] = back.astype(jnp.bfloat16)

    def compute(s):
        count = 4 if 0 < s < half else 2

        @pl.loop(0, count)
        def _(t):
            sign = 2 * lax.div(t, 2) - 1
            consume(2 * chip_at(p + s * sign) + lax.rem(t, 2))

    share_start(0)
    load.wait()
    for way in range(2):
        go(ring_copy(way, 1, f))
    own = remote(w_all.at[f], w_all.at[f], own_send, own_recv, sibling)
    go(own)

    live = (tenant[...] >= 0).astype(jnp.float32)
    size = live.shape[1]
    diagonal = lax.broadcasted_iota(jnp.int32, (size, size), 0) == lax.broadcasted_iota(
        jnp.int32, (size, size), 1
    )
    live_col[...] = jnp.sum(
        jnp.where(diagonal, jnp.broadcast_to(live, (size, size)), 0.0), axis=1, keepdims=True
    )
    mg[...] = (grad[...].astype(jnp.float32) * live_col[...]).astype(jnp.bfloat16)
    tenants = table.shape[0]

    @pl.loop(0, n)
    def _(b):
        tenant_of = lax.fori_loop(
            0,
            tenants,
            lambda t, count: count + (offsets[t + 1] <= b * BLOCK).astype(jnp.int32),
            jnp.int32(0),
        )
        slots[b] = table[jnp.minimum(tenant_of, tenants - 1)]

    share_wait(0)

    @pl.loop(0, n)
    def _(b):
        share_out[1, b] = share_in0[slots[b]]

    share_start(1)
    pass_on(1)
    share_wait(1)

    rank = down.shape[1]
    shrunk = jnp.zeros((rank, size), jnp.float32)
    pulled = jnp.zeros((rank, size), jnp.float32)
    for j in range(n):
        shrunk += lax.dot_general(
            share_in1[j, :, :width],
            acts[:, j * width : (j + 1) * width],
            LAST,
            preferred_element_type=jnp.float32,
        )
    for k in range(ups):
        pulled += lax.dot_general(
            share_in1[k, :, width:],
            mg[:, k * LANES : (k + 1) * LANES],
            LAST,
            preferred_element_type=jnp.float32,
        )
    scale = adapter_scale_factor
    shrunk2_f32 = shrunk.astype(jnp.bfloat16).astype(jnp.float32) * scale
    pulled2_f32 = pulled.astype(jnp.bfloat16).astype(jnp.float32) * scale
    shrunk2_t = shrunk2_f32.astype(jnp.bfloat16)
    pulled2_t = pulled2_f32.astype(jnp.bfloat16)
    shrunk2 = shrunk2_f32.T.astype(jnp.bfloat16)
    pulled2[...] = pulled2_f32.T.astype(jnp.bfloat16)
    for j in range(n):
        share_out[2, j, :, :width] = jnp.dot(
            pulled2_t, acts[:, j * width : (j + 1) * width], preferred_element_type=jnp.float32
        ).astype(jnp.bfloat16)
    for k in range(ups):
        columns = slice(k * LANES, (k + 1) * LANES)
        term = jnp.dot(shrunk2_t, mg[:, columns], preferred_element_type=jnp.float32).astype(
            jnp.bfloat16
        )
        for j in range(k, n, ups):
            share_out[2, j, :, width:] = term
        total[:, columns] = jnp.dot(
            shrunk2, share_in1[k, :, width:], preferred_element_type=jnp.float32
        )
    share_start(2)
    remote(
        w_all.at[2 * chip + 1 - core], w_all.at[2 * chip + 1 - core], own_send, own_recv, sibling
    ).wait_recv()
    compute(0)
    for s in range(2, half + 1):
        pass_on(s)
        if s == 2:
            share_wait(2)

            @pl.loop(0, n)
            def _(slot):
                summed = jnp.zeros(share_in2.shape[1:], jnp.float32)
                for b in range(n):
                    summed += jnp.where(
                        slots[b] == slot, share_in2[b].astype(jnp.float32), 0.0
                    )
                share_out[3, slot] = summed.astype(jnp.bfloat16)

            share_start(3)
        finish(s - 1)
        compute(s - 1)
    share_wait(3)
    for j in range(n):
        down_grad[0, :, j * width : (j + 1) * width] = share_in3[j, :, :width].astype(jnp.float32)
    for k in range(ups):
        up_grad[0, :, k * LANES : (k + 1) * LANES] = share_in3[k, :, width:].astype(jnp.float32)
    finish(half)
    compute(half)
    out[...] = (total[...] * live_col[...]).astype(jnp.bfloat16)
    for copy in sends:
        copy.wait_send()
    for phase in range(4):

        @pl.loop(1, n)
        def _(d):
            share_copy(phase, lax.rem(f + d, n), f).wait_send()


def fused(
    activations,
    grad_out,
    token_tenant,
    segment_offsets,
    value_weight,
    down_weight_pool,
    up_weight_pool,
    page_table,
):
    n = lax.axis_size("fsdp")
    tokens, model = activations.shape
    rows, out_width = value_weight.shape
    rank = down_weight_pool.shape[1]
    steps = n // 4
    vmem = pl.BlockSpec(memory_space=pltpu.VMEM)
    smem = pl.BlockSpec(memory_space=pltpu.SMEM)
    dma = pltpu.SemaphoreType.DMA
    return pl.pallas_call(
        functools.partial(fused_kernel, n),
        out_shape=(
            jax.ShapeDtypeStruct((tokens, out_width), jnp.bfloat16),
            jax.ShapeDtypeStruct((tokens, model), jnp.bfloat16),
            jax.ShapeDtypeStruct((1, rank, model), jnp.float32),
            jax.ShapeDtypeStruct((1, rank, out_width), jnp.float32),
        ),
        in_specs=[vmem, vmem, vmem, smem, smem, pl.BlockSpec(memory_space=pl.ANY), vmem, vmem],
        out_specs=[vmem] * 4,
        scratch_shapes=[
            pltpu.VMEM((n, rows, out_width), jnp.bfloat16),
            pltpu.VMEM((tokens, out_width), jnp.bfloat16),
            pltpu.VMEM((tokens, out_width), jnp.float32),
            pltpu.VMEM((4, n, rank, model // n + LANES), jnp.bfloat16),
            pltpu.VMEM((n, rank, model // n + LANES), jnp.bfloat16),
            pltpu.VMEM((n, rank, model // n + LANES), jnp.bfloat16),
            pltpu.VMEM((n, rank, model // n + LANES), jnp.bfloat16),
            pltpu.VMEM((n, rank, model // n + LANES), jnp.bfloat16),
            pltpu.SMEM((n,), jnp.int32),
            pltpu.VMEM((tokens, rank), jnp.bfloat16),
            pltpu.VMEM((tokens, 1), jnp.float32),
            dma,
        ]
        + [dma((2, steps))] * 8
        + [dma, dma, dma((4, n)), dma((4, n))],
        compiler_params=pltpu.CompilerParams(
            collective_id=0, has_side_effects=True, vmem_limit_bytes=56 * 2**20
        ),
        cost_estimate=pl.CostEstimate(
            flops=4 * tokens * model * out_width,
            bytes_accessed=4 * tokens * model + 4 * model * out_width // n,
            transcendentals=0,
        ),
    )(
        activations,
        grad_out,
        token_tenant.reshape(1, tokens),
        segment_offsets,
        page_table,
        value_weight,
        down_weight_pool,
        up_weight_pool,
    )


def either(*args):
    n = lax.axis_size("fsdp")
    tokens, model = args[0].shape
    rows, out_width = args[4].shape
    slots, rank = args[5].shape[:2]
    fits = (
        lax.axis_size("groups") == 2
        and n % 8 == 0
        and n <= 32
        and tokens == BLOCK
        and slots == 1
        and rank % 16 == 0
        and model % (n * LANES) == 0
        and out_width % LANES == 0
        and out_width // LANES <= n
        and rows >= 128
        and rows % 16 == 0
    )
    return (fused if fits else on_device)(*args)


def solution(mesh):
    placed = (
        P(("groups", "fsdp"), None),
        P(("groups", "fsdp"), None),
        P(("groups", "fsdp")),
        P("groups"),
        P("fsdp", None),
        P("fsdp", None, None),
        P("fsdp", None, None),
        P(),
    )
    return jax.shard_map(
        either,
        mesh=mesh,
        in_specs=placed,
        out_specs=(
            P(("groups", "fsdp"), None),
            P(("groups", "fsdp"), None),
            P(("groups", "fsdp"), None, None),
            P(("groups", "fsdp"), None, None),
        ),
        check_vma=False,
    )
```

```python
import functools

import jax
import jax.numpy as jnp
from jax import lax
from jax.experimental import pallas as pl
from jax.experimental.pallas import tpu as pltpu
from jax.sharding import PartitionSpec as P

BLOCK = 128


adapter_scale_factor = 2.0


def on_device(
    activations,
    grad_out,
    token_tenant,
    segment_offsets,
    value_weight,
    down_weight_pool,
    up_weight_pool,
    page_table,
):
    devices = lax.axis_size("fsdp")
    tok_rows, hidden_model_width = activations.shape
    output_width = grad_out.shape[1]
    local_slot_count = down_weight_pool.shape[0]
    adapter_rank_size = down_weight_pool.shape[1]
    tenants = page_table.shape[0]
    local_block_count = tok_rows // BLOCK
    blocks_all = local_block_count * devices
    active_token_rows = token_tenant >= 0
    masked_grad = grad_out * active_token_rows.astype(jnp.bfloat16)[:, None]
    contract_last = (((1,), (1,)), ((), ()))
    full_weight = lax.all_gather(value_weight, "fsdp", axis=0, tiled=True)
    base_output_rows = jnp.dot(activations, full_weight, preferred_element_type=jnp.float32)
    base_gradient_input = lax.dot_general(
        masked_grad, full_weight, contract_last, preferred_element_type=jnp.float32
    )
    flattened_down_weight = down_weight_pool.reshape(
        local_slot_count, adapter_rank_size * hidden_model_width
    )
    flattened_up_weight = up_weight_pool.reshape(local_slot_count, adapter_rank_size * output_width)
    held_down, held_up = (
        lax.all_to_all(flattened_down_weight, "fsdp", split_axis=1, concat_axis=0, tiled=True),
        lax.all_to_all(flattened_up_weight, "fsdp", split_axis=1, concat_axis=0, tiled=True),
    )
    share_down = held_down.shape[1]
    share_up = held_up.shape[1]
    block_first = lax.iota(jnp.int32, blocks_all) * BLOCK
    block_tenant = jnp.sum(
        (segment_offsets[1:][None, :] <= block_first[:, None]).astype(jnp.int32), axis=1
    )
    tenant_match = block_tenant[:, None] == lax.iota(jnp.int32, tenants)[None, :]
    block_slot = jnp.sum(jnp.where(tenant_match, page_table[None, :], 0), axis=1)
    send_down = jnp.take(held_down, block_slot, axis=0).reshape(
        devices, local_block_count, share_down
    )
    send_up = jnp.take(held_up, block_slot, axis=0).reshape(devices, local_block_count, share_up)
    fetched_down_weight, fetched_up_weight = (
        lax.all_to_all(send_down, "fsdp", split_axis=0, concat_axis=2, tiled=True),
        lax.all_to_all(send_up, "fsdp", split_axis=0, concat_axis=2, tiled=True),
    )
    down_weight_block = fetched_down_weight.reshape(
        local_block_count, adapter_rank_size, hidden_model_width
    )
    up_weight_block = fetched_up_weight.reshape(local_block_count, adapter_rank_size, output_width)
    input_blocks = activations.reshape(local_block_count, BLOCK, hidden_model_width)
    gradient_blocks = masked_grad.reshape(local_block_count, BLOCK, output_width)
    reduced_rank_rows = jnp.einsum(
        "bnd,brd->bnr", input_blocks, down_weight_block, preferred_element_type=jnp.float32
    ).astype(jnp.bfloat16)
    expanded_rows = jnp.einsum(
        "bnr,bro->bno", reduced_rank_rows, up_weight_block, preferred_element_type=jnp.float32
    ).reshape(tok_rows, output_width)
    pulled_rows = jnp.einsum(
        "bno,bro->bnr", gradient_blocks, up_weight_block, preferred_element_type=jnp.float32
    ).astype(jnp.bfloat16)
    scattered_gradient = jnp.einsum(
        "bnr,brd->bnd", pulled_rows, down_weight_block, preferred_element_type=jnp.float32
    ).reshape(tok_rows, hidden_model_width)
    adapted_value_output = (
        (base_output_rows + adapter_scale_factor * expanded_rows)
        * active_token_rows.astype(jnp.float32)[:, None]
    ).astype(jnp.bfloat16)
    input_gradient = (base_gradient_input + adapter_scale_factor * scattered_gradient).astype(
        jnp.bfloat16
    )
    down_weight_terms = adapter_scale_factor * jnp.einsum(
        "kpz,kpj->kzj", pulled_rows, input_blocks, preferred_element_type=jnp.float32
    )
    up_weight_terms = adapter_scale_factor * jnp.einsum(
        "yig,yiw->ygw", reduced_rank_rows, gradient_blocks, preferred_element_type=jnp.float32
    )
    ret_down = down_weight_terms.reshape(local_block_count, devices, share_down)
    ret_up = up_weight_terms.reshape(local_block_count, devices, share_up)
    back_down, back_up = (
        lax.all_to_all(ret_down, "fsdp", split_axis=1, concat_axis=0, tiled=True),
        lax.all_to_all(ret_up, "fsdp", split_axis=1, concat_axis=0, tiled=True),
    )
    recv_down = back_down.reshape(blocks_all, share_down)
    recv_up = back_up.reshape(blocks_all, share_up)
    slot_match = (block_slot[None, :] == lax.iota(jnp.int32, tenants)[:, None]).astype(jnp.float32)
    sum_down = jnp.dot(
        slot_match, recv_down, precision=lax.Precision.HIGHEST, preferred_element_type=jnp.float32
    )
    sum_up = jnp.dot(
        slot_match, recv_up, precision=lax.Precision.HIGHEST, preferred_element_type=jnp.float32
    )
    resident_down_weight, resident_up_weight = (
        lax.all_to_all(sum_down, "fsdp", split_axis=0, concat_axis=1, tiled=True),
        lax.all_to_all(sum_up, "fsdp", split_axis=0, concat_axis=1, tiled=True),
    )
    down_pool_gradient = resident_down_weight.reshape(
        local_slot_count, adapter_rank_size, hidden_model_width
    )
    up_pool_gradient = resident_up_weight.reshape(local_slot_count, adapter_rank_size, output_width)
    return (adapted_value_output, input_gradient, down_pool_gradient, up_pool_gradient)


LAST = (((1,), (1,)), ((), ()))
FIRST = (((0,), (0,)), ((), ()))
LANES = 128


def remote(src, dst, send, recv, where):
    return pltpu.make_async_remote_copy(
        src_ref=src,
        dst_ref=dst,
        send_sem=send,
        recv_sem=recv,
        device_id=where,
        device_id_type=pl.DeviceIdType.MESH,
    )


def fused_kernel(
    n,
    acts,
    grad,
    tenant,
    offsets,
    table,
    w_hbm,
    down,
    up,
    out,
    ig,
    down_grad,
    up_grad,
    w_all,
    mg,
    total,
    share_out,
    share_in0,
    share_in1,
    share_in2,
    share_in3,
    slots,
    pulled2,
    live_col,
    local_sem,
    ring_send,
    ring_recv,
    x_send,
    x_recv,
    core_send,
    core_recv,
    corex_send,
    corex_recv,
    own_send,
    own_recv,
    share_send,
    share_recv,
):
    share_in = (share_in0, share_in1, share_in2, share_in3)
    x = lax.axis_index("groups")
    f = lax.axis_index("fsdp")
    m = n // 2
    half = m // 2
    chip, core = lax.div(f, 2), lax.rem(f, 2)
    z, y = lax.div(chip, 2), lax.rem(chip, 2)
    p = z + y * (m - 1 - 2 * z)
    width = down.shape[2] // n
    out_width = up.shape[2]
    ups = out_width // LANES
    rows = w_all.shape[1]
    cut = ((rows * 176) // 512) // 16 * 16
    length = rows - cut

    def chip_at(position):
        q = lax.rem(position + 2 * m, m)
        y_q = lax.div(q, half)
        return 2 * (q + y_q * (m - 1 - 2 * q)) + y_q

    def at(shard, start, size):
        return w_all.at[shard, pl.ds(pl.multiple_of(start, 16), size), :]

    right = {"fsdp": 2 * chip_at(p + 1) + core}
    left = {"fsdp": 2 * chip_at(p - 1) + core}
    sibling = {"fsdp": 2 * chip + 1 - core}
    across = {"groups": 1 - x}
    mine_start = x * length
    other_start = (1 - x) * length

    barrier = pltpu.get_barrier_semaphore()

    @pl.loop(1, n)
    def _(d):
        pl.semaphore_signal(
            barrier,
            inc=1,
            device_id={"fsdp": lax.rem(f + d, n)},
            device_id_type=pl.DeviceIdType.MESH,
        )

    pl.semaphore_signal(barrier, inc=1, device_id=across, device_id_type=pl.DeviceIdType.MESH)
    load = pltpu.make_async_copy(w_hbm, w_all.at[f], local_sem)
    load.start()
    for j in range(n):
        share_out[0, j, :, :width] = down[0, :, j * width : (j + 1) * width]
        k = j % ups
        share_out[0, j, :, width:] = up[0, :, k * LANES : (k + 1) * LANES]
    pl.semaphore_wait(barrier, n)

    def share_copy(phase, j, slot):
        return remote(
            share_out.at[phase, j],
            share_in[phase].at[slot],
            share_send.at[phase, j],
            share_recv.at[phase, slot],
            {"fsdp": j},
        )

    def share_start(phase):
        @pl.loop(1, n)
        def _(d):
            j = lax.rem(f + d, n)
            share_copy(phase, j, f).start()

        share_in[phase][f] = share_out[phase, f]

    def share_wait(phase):
        @pl.loop(1, n)
        def _(d):
            j = lax.rem(f + d, n)
            share_copy(phase, j, j).wait_recv()

    sends = []

    def go(copy):
        copy.start()
        sends.append(copy)

    def ring_copy(way, s, piece, shard):
        if piece == 0:
            part = at(shard, mine_start, cut)
        else:
            part = at(shard, cut, length - cut)
        return remote(
            part,
            part,
            ring_send.at[way, s - 1, piece],
            ring_recv.at[way, s - 1, piece],
            (right, left)[way],
        )

    def x_copy(way, s, shard, start):
        part = at(shard, start, cut)
        return remote(part, part, x_send.at[way, s - 1], x_recv.at[way, s - 1], across)

    def core_copy(way, s, piece, shard):
        if piece == 0:
            part = at(shard, mine_start, cut)
        else:
            part = at(shard, cut, length - cut)
        return remote(
            part,
            part,
            core_send.at[way, s - 1, piece],
            core_recv.at[way, s - 1, piece],
            sibling,
        )

    def corex_copy(way, s, shard):
        part = at(shard, other_start, cut)
        return remote(part, part, corex_send.at[way, s - 1], corex_recv.at[way, s - 1], sibling)

    def shard_of(way, s, c):
        return 2 * chip_at(p - s if way == 0 else p + s) + c

    def pass_on(s, piece):
        for way in range(2) if s < half else (piece,):
            shard = shard_of(way, s, core)
            ring_copy(way, s, piece, shard).wait_recv()
            if s + 1 < half or (s + 1 == half and way == piece):
                go(ring_copy(way, s + 1, piece, shard))
            slot = way if s < half else 0
            if piece == 0:
                go(x_copy(slot, s, shard, mine_start))
            go(core_copy(slot, s, piece, shard))

    def finish(s):
        ways = 2 if s < half else 1
        for way in range(ways):
            shard = shard_of(way, s, core)
            x_copy(way, s, shard, other_start).wait_recv()
            go(corex_copy(way, s, shard))
        for way in range(ways):
            shard = shard_of(way, s, 1 - core)
            for piece in range(2):
                core_copy(way, s, piece, shard).wait_recv()
            corex_copy(way, s, shard).wait_recv()

    def consume(shard):
        columns = pl.ds(pl.multiple_of(shard * width, LANES), width)
        w = w_all[shard]
        total[...] += jnp.dot(acts[:, columns], w, preferred_element_type=jnp.float32)
        back = lax.dot_general(mg[...], w, LAST, preferred_element_type=jnp.float32)
        back += jnp.dot(
            pulled2[...], share_in1[shard, :, :width], preferred_element_type=jnp.float32
        )
        ig[:, columns] = back.astype(jnp.bfloat16)

    def compute(s):
        count = 4 if 0 < s < half else 2

        @pl.loop(0, count)
        def _(t):
            sign = 2 * lax.div(t, 2) - 1
            consume(2 * chip_at(p + s * sign) + lax.rem(t, 2))

    share_start(0)
    load.wait()
    for piece in range(2):
        for way in range(2):
            go(ring_copy(way, 1, piece, f))
    own = remote(w_all.at[f], w_all.at[f], own_send, own_recv, sibling)
    go(own)

    live = (tenant[...] >= 0).astype(jnp.float32)
    size = live.shape[1]
    diagonal = lax.broadcasted_iota(jnp.int32, (size, size), 0) == lax.broadcasted_iota(
        jnp.int32, (size, size), 1
    )
    live_col[...] = jnp.sum(
        jnp.where(diagonal, jnp.broadcast_to(live, (size, size)), 0.0), axis=1, keepdims=True
    )
    mg[...] = (grad[...].astype(jnp.float32) * live_col[...]).astype(jnp.bfloat16)
    tenants = table.shape[0]

    @pl.loop(0, n)
    def _(b):
        tenant_of = lax.fori_loop(
            0,
            tenants,
            lambda t, count: count + (offsets[t + 1] <= b * BLOCK).astype(jnp.int32),
            jnp.int32(0),
        )
        slots[b] = table[jnp.minimum(tenant_of, tenants - 1)]

    pass_on(1, 0)
    pass_on(1, 1)
    share_wait(0)

    @pl.loop(0, n)
    def _(b):
        share_out[1, b] = share_in0[slots[b]]

    share_start(1)
    pass_on(2, 0)
    pass_on(2, 1)
    share_wait(1)

    rank = down.shape[1]
    shrunk = jnp.zeros((rank, size), jnp.float32)
    pulled = jnp.zeros((rank, size), jnp.float32)
    for j in range(n):
        shrunk += lax.dot_general(
            share_in1[j, :, :width],
            acts[:, j * width : (j + 1) * width],
            LAST,
            preferred_element_type=jnp.float32,
        )
    for k in range(ups):
        pulled += lax.dot_general(
            share_in1[k, :, width:],
            mg[:, k * LANES : (k + 1) * LANES],
            LAST,
            preferred_element_type=jnp.float32,
        )
    scale = adapter_scale_factor
    shrunk2_f32 = shrunk.astype(jnp.bfloat16).astype(jnp.float32) * scale
    pulled2_f32 = pulled.astype(jnp.bfloat16).astype(jnp.float32) * scale
    shrunk2_t = shrunk2_f32.astype(jnp.bfloat16)
    pulled2_t = pulled2_f32.astype(jnp.bfloat16)
    shrunk2 = shrunk2_f32.T.astype(jnp.bfloat16)
    pulled2[...] = pulled2_f32.T.astype(jnp.bfloat16)
    for j in range(n):
        share_out[2, j, :, :width] = jnp.dot(
            pulled2_t, acts[:, j * width : (j + 1) * width], preferred_element_type=jnp.float32
        ).astype(jnp.bfloat16)
    for k in range(ups):
        columns = slice(k * LANES, (k + 1) * LANES)
        term = jnp.dot(shrunk2_t, mg[:, columns], preferred_element_type=jnp.float32).astype(
            jnp.bfloat16
        )
        for j in range(k, n, ups):
            share_out[2, j, :, width:] = term
        total[:, columns] = jnp.dot(
            shrunk2, share_in1[k, :, width:], preferred_element_type=jnp.float32
        )
    share_start(2)
    remote(
        w_all.at[2 * chip + 1 - core], w_all.at[2 * chip + 1 - core], own_send, own_recv, sibling
    ).wait_recv()
    compute(0)
    finish(1)
    compute(1)
    pass_on(3, 0)
    pass_on(3, 1)
    share_wait(2)

    @pl.loop(0, n)
    def _(slot):
        summed = jnp.zeros(share_in2.shape[1:], jnp.float32)
        for b in range(n):
            summed += jnp.where(slots[b] == slot, share_in2[b].astype(jnp.float32), 0.0)
        share_out[3, slot] = summed.astype(jnp.bfloat16)

    share_start(3)
    finish(2)
    compute(2)
    for s in range(3, half):
        pass_on(s + 1, 0)
        pass_on(s + 1, 1)
        finish(s)
        compute(s)
    share_wait(3)
    for j in range(n):
        down_grad[0, :, j * width : (j + 1) * width] = share_in3[j, :, :width].astype(jnp.float32)
    for k in range(ups):
        up_grad[0, :, k * LANES : (k + 1) * LANES] = share_in3[k, :, width:].astype(jnp.float32)
    finish(half)
    compute(half)
    out[...] = (total[...] * live_col[...]).astype(jnp.bfloat16)
    for copy in sends:
        copy.wait_send()
    for phase in range(4):

        @pl.loop(1, n)
        def _(d):
            share_copy(phase, lax.rem(f + d, n), f).wait_send()


def fused(
    activations,
    grad_out,
    token_tenant,
    segment_offsets,
    value_weight,
    down_weight_pool,
    up_weight_pool,
    page_table,
):
    n = lax.axis_size("fsdp")
    tokens, model = activations.shape
    rows, out_width = value_weight.shape
    rank = down_weight_pool.shape[1]
    steps = n // 4
    vmem = pl.BlockSpec(memory_space=pltpu.VMEM)
    smem = pl.BlockSpec(memory_space=pltpu.SMEM)
    dma = pltpu.SemaphoreType.DMA
    return pl.pallas_call(
        functools.partial(fused_kernel, n),
        out_shape=(
            jax.ShapeDtypeStruct((tokens, out_width), jnp.bfloat16),
            jax.ShapeDtypeStruct((tokens, model), jnp.bfloat16),
            jax.ShapeDtypeStruct((1, rank, model), jnp.float32),
            jax.ShapeDtypeStruct((1, rank, out_width), jnp.float32),
        ),
        in_specs=[vmem, vmem, vmem, smem, smem, pl.BlockSpec(memory_space=pl.ANY), vmem, vmem],
        out_specs=[vmem] * 4,
        scratch_shapes=[
            pltpu.VMEM((n, rows, out_width), jnp.bfloat16),
            pltpu.VMEM((tokens, out_width), jnp.bfloat16),
            pltpu.VMEM((tokens, out_width), jnp.float32),
            pltpu.VMEM((4, n, rank, model // n + LANES), jnp.bfloat16),
            pltpu.VMEM((n, rank, model // n + LANES), jnp.bfloat16),
            pltpu.VMEM((n, rank, model // n + LANES), jnp.bfloat16),
            pltpu.VMEM((n, rank, model // n + LANES), jnp.bfloat16),
            pltpu.VMEM((n, rank, model // n + LANES), jnp.bfloat16),
            pltpu.SMEM((n,), jnp.int32),
            pltpu.VMEM((tokens, rank), jnp.bfloat16),
            pltpu.VMEM((tokens, 1), jnp.float32),
            dma,
        ]
        + [dma((2, steps, 2))] * 2
        + [dma((2, steps))] * 2
        + [dma((2, steps, 2))] * 2
        + [dma((2, steps))] * 2
        + [dma, dma, dma((4, n)), dma((4, n))],
        compiler_params=pltpu.CompilerParams(
            collective_id=0, has_side_effects=True, vmem_limit_bytes=56 * 2**20
        ),
        cost_estimate=pl.CostEstimate(
            flops=4 * tokens * model * out_width,
            bytes_accessed=4 * tokens * model + 4 * model * out_width // n,
            transcendentals=0,
        ),
    )(
        activations,
        grad_out,
        token_tenant.reshape(1, tokens),
        segment_offsets,
        page_table,
        value_weight,
        down_weight_pool,
        up_weight_pool,
    )


def either(*args):
    n = lax.axis_size("fsdp")
    tokens, model = args[0].shape
    rows, out_width = args[4].shape
    slots, rank = args[5].shape[:2]
    fits = (
        lax.axis_size("groups") == 2
        and n % 8 == 0
        and n <= 32
        and tokens == BLOCK
        and slots == 1
        and rank % 16 == 0
        and model % (n * LANES) == 0
        and out_width % LANES == 0
        and out_width // LANES <= n
        and rows >= 128
        and rows % 16 == 0
    )
    return (fused if fits else on_device)(*args)


def solution(mesh):
    placed = (
        P(("groups", "fsdp"), None),
        P(("groups", "fsdp"), None),
        P(("groups", "fsdp")),
        P("groups"),
        P("fsdp", None),
        P("fsdp", None, None),
        P("fsdp", None, None),
        P(),
    )
    return jax.shard_map(
        either,
        mesh=mesh,
        in_specs=placed,
        out_specs=(
            P(("groups", "fsdp"), None),
            P(("groups", "fsdp"), None),
            P(("groups", "fsdp"), None, None),
            P(("groups", "fsdp"), None, None),
        ),
        check_vma=False,
    )
```

```python
import functools

import jax
import jax.numpy as jnp
from jax import lax
from jax.experimental import pallas as pl
from jax.experimental.pallas import tpu as pltpu
from jax.sharding import PartitionSpec as P

BLOCK = 128


adapter_scale_factor = 2.0


def on_device(
    activations,
    grad_out,
    token_tenant,
    segment_offsets,
    value_weight,
    down_weight_pool,
    up_weight_pool,
    page_table,
):
    devices = lax.axis_size("fsdp")
    tok_rows, hidden_model_width = activations.shape
    output_width = grad_out.shape[1]
    local_slot_count = down_weight_pool.shape[0]
    adapter_rank_size = down_weight_pool.shape[1]
    tenants = page_table.shape[0]
    local_block_count = tok_rows // BLOCK
    blocks_all = local_block_count * devices
    active_token_rows = token_tenant >= 0
    masked_grad = grad_out * active_token_rows.astype(jnp.bfloat16)[:, None]
    contract_last = (((1,), (1,)), ((), ()))
    full_weight = lax.all_gather(value_weight, "fsdp", axis=0, tiled=True)
    base_output_rows = jnp.dot(activations, full_weight, preferred_element_type=jnp.float32)
    base_gradient_input = lax.dot_general(
        masked_grad, full_weight, contract_last, preferred_element_type=jnp.float32
    )
    flattened_down_weight = down_weight_pool.reshape(
        local_slot_count, adapter_rank_size * hidden_model_width
    )
    flattened_up_weight = up_weight_pool.reshape(local_slot_count, adapter_rank_size * output_width)
    held_down, held_up = (
        lax.all_to_all(flattened_down_weight, "fsdp", split_axis=1, concat_axis=0, tiled=True),
        lax.all_to_all(flattened_up_weight, "fsdp", split_axis=1, concat_axis=0, tiled=True),
    )
    share_down = held_down.shape[1]
    share_up = held_up.shape[1]
    block_first = lax.iota(jnp.int32, blocks_all) * BLOCK
    block_tenant = jnp.sum(
        (segment_offsets[1:][None, :] <= block_first[:, None]).astype(jnp.int32), axis=1
    )
    tenant_match = block_tenant[:, None] == lax.iota(jnp.int32, tenants)[None, :]
    block_slot = jnp.sum(jnp.where(tenant_match, page_table[None, :], 0), axis=1)
    send_down = jnp.take(held_down, block_slot, axis=0).reshape(
        devices, local_block_count, share_down
    )
    send_up = jnp.take(held_up, block_slot, axis=0).reshape(devices, local_block_count, share_up)
    fetched_down_weight, fetched_up_weight = (
        lax.all_to_all(send_down, "fsdp", split_axis=0, concat_axis=2, tiled=True),
        lax.all_to_all(send_up, "fsdp", split_axis=0, concat_axis=2, tiled=True),
    )
    down_weight_block = fetched_down_weight.reshape(
        local_block_count, adapter_rank_size, hidden_model_width
    )
    up_weight_block = fetched_up_weight.reshape(local_block_count, adapter_rank_size, output_width)
    input_blocks = activations.reshape(local_block_count, BLOCK, hidden_model_width)
    gradient_blocks = masked_grad.reshape(local_block_count, BLOCK, output_width)
    reduced_rank_rows = jnp.einsum(
        "bnd,brd->bnr", input_blocks, down_weight_block, preferred_element_type=jnp.float32
    ).astype(jnp.bfloat16)
    expanded_rows = jnp.einsum(
        "bnr,bro->bno", reduced_rank_rows, up_weight_block, preferred_element_type=jnp.float32
    ).reshape(tok_rows, output_width)
    pulled_rows = jnp.einsum(
        "bno,bro->bnr", gradient_blocks, up_weight_block, preferred_element_type=jnp.float32
    ).astype(jnp.bfloat16)
    scattered_gradient = jnp.einsum(
        "bnr,brd->bnd", pulled_rows, down_weight_block, preferred_element_type=jnp.float32
    ).reshape(tok_rows, hidden_model_width)
    adapted_value_output = (
        (base_output_rows + adapter_scale_factor * expanded_rows)
        * active_token_rows.astype(jnp.float32)[:, None]
    ).astype(jnp.bfloat16)
    input_gradient = (base_gradient_input + adapter_scale_factor * scattered_gradient).astype(
        jnp.bfloat16
    )
    down_weight_terms = adapter_scale_factor * jnp.einsum(
        "kpz,kpj->kzj", pulled_rows, input_blocks, preferred_element_type=jnp.float32
    )
    up_weight_terms = adapter_scale_factor * jnp.einsum(
        "yig,yiw->ygw", reduced_rank_rows, gradient_blocks, preferred_element_type=jnp.float32
    )
    ret_down = down_weight_terms.reshape(local_block_count, devices, share_down)
    ret_up = up_weight_terms.reshape(local_block_count, devices, share_up)
    back_down, back_up = (
        lax.all_to_all(ret_down, "fsdp", split_axis=1, concat_axis=0, tiled=True),
        lax.all_to_all(ret_up, "fsdp", split_axis=1, concat_axis=0, tiled=True),
    )
    recv_down = back_down.reshape(blocks_all, share_down)
    recv_up = back_up.reshape(blocks_all, share_up)
    slot_match = (block_slot[None, :] == lax.iota(jnp.int32, tenants)[:, None]).astype(jnp.float32)
    sum_down = jnp.dot(
        slot_match, recv_down, precision=lax.Precision.HIGHEST, preferred_element_type=jnp.float32
    )
    sum_up = jnp.dot(
        slot_match, recv_up, precision=lax.Precision.HIGHEST, preferred_element_type=jnp.float32
    )
    resident_down_weight, resident_up_weight = (
        lax.all_to_all(sum_down, "fsdp", split_axis=0, concat_axis=1, tiled=True),
        lax.all_to_all(sum_up, "fsdp", split_axis=0, concat_axis=1, tiled=True),
    )
    down_pool_gradient = resident_down_weight.reshape(
        local_slot_count, adapter_rank_size, hidden_model_width
    )
    up_pool_gradient = resident_up_weight.reshape(local_slot_count, adapter_rank_size, output_width)
    return (adapted_value_output, input_gradient, down_pool_gradient, up_pool_gradient)


LAST = (((1,), (1,)), ((), ()))
FIRST = (((0,), (0,)), ((), ()))
LANES = 128


def remote(src, dst, send, recv, where):
    return pltpu.make_async_remote_copy(
        src_ref=src,
        dst_ref=dst,
        send_sem=send,
        recv_sem=recv,
        device_id=where,
        device_id_type=pl.DeviceIdType.MESH,
    )


def fused_kernel(
    n,
    acts_hbm,
    grad,
    tenant,
    offsets,
    table,
    w_hbm,
    down,
    up,
    out,
    ig_hbm,
    down_grad,
    up_grad,
    w_all,
    mg,
    total,
    share_out,
    share_in0,
    share_in1,
    share_in2,
    share_in3,
    slots,
    pulled2,
    live_col,
    acts,
    ig,
    acts_sem,
    ig_sem,
    local_sem,
    ring_send,
    ring_recv,
    x_send,
    x_recv,
    core_send,
    core_recv,
    corex_send,
    corex_recv,
    own_send,
    own_recv,
    share_send,
    share_recv,
):
    share_in = (share_in0, share_in1, share_in2, share_in3)
    x = lax.axis_index("groups")
    f = lax.axis_index("fsdp")
    m = n // 2
    half = m // 2
    chip, core = lax.div(f, 2), lax.rem(f, 2)
    z, y = lax.div(chip, 2), lax.rem(chip, 2)
    p = z + y * (m - 1 - 2 * z)
    width = down.shape[2] // n
    out_width = up.shape[2]
    ups = out_width // LANES
    rows = w_all.shape[1]
    cut = ((rows * 208) // 512) // 16 * 16
    length = rows - cut

    def chip_at(position):
        q = lax.rem(position + 2 * m, m)
        y_q = lax.div(q, half)
        return 2 * (q + y_q * (m - 1 - 2 * q)) + y_q

    def at(shard, start, size):
        return w_all.at[shard, pl.ds(pl.multiple_of(start, 16), size), :]

    right = {"fsdp": 2 * chip_at(p + 1) + core}
    left = {"fsdp": 2 * chip_at(p - 1) + core}
    sibling = {"fsdp": 2 * chip + 1 - core}
    across = {"groups": 1 - x}
    mine_start = x * length
    other_start = (1 - x) * length

    barrier = pltpu.get_barrier_semaphore()

    @pl.loop(1, n)
    def _(d):
        pl.semaphore_signal(
            barrier,
            inc=1,
            device_id={"fsdp": lax.rem(f + d, n)},
            device_id_type=pl.DeviceIdType.MESH,
        )

    pl.semaphore_signal(barrier, inc=1, device_id=across, device_id_type=pl.DeviceIdType.MESH)
    fetch = pltpu.make_async_copy(acts_hbm, acts, acts_sem)
    load = pltpu.make_async_copy(w_hbm, w_all.at[f], local_sem)
    load.start()
    fetch.start()
    for j in range(n):
        share_out[0, j, :, :width] = down[0, :, j * width : (j + 1) * width]
        k = j % ups
        share_out[0, j, :, width:] = up[0, :, k * LANES : (k + 1) * LANES]
    pl.semaphore_wait(barrier, n)

    def share_copy(phase, j, slot):
        return remote(
            share_out.at[phase, j],
            share_in[phase].at[slot],
            share_send.at[phase, j],
            share_recv.at[phase, slot],
            {"fsdp": j},
        )

    def share_start(phase):
        @pl.loop(1, n)
        def _(d):
            j = lax.rem(f + d, n)
            share_copy(phase, j, f).start()

        share_in[phase][f] = share_out[phase, f]

    def share_wait(phase):
        @pl.loop(1, n)
        def _(d):
            j = lax.rem(f + d, n)
            share_copy(phase, j, j).wait_recv()

    sends = []

    def go(copy):
        copy.start()
        sends.append(copy)

    def ring_copy(way, s, piece, shard):
        if piece == 0:
            part = at(shard, mine_start, cut)
        else:
            part = at(shard, cut, length - cut)
        return remote(
            part,
            part,
            ring_send.at[way, s - 1, piece],
            ring_recv.at[way, s - 1, piece],
            (right, left)[way],
        )

    def x_copy(way, s, shard, start):
        part = at(shard, start, cut)
        return remote(part, part, x_send.at[way, s - 1], x_recv.at[way, s - 1], across)

    def core_copy(way, s, piece, shard):
        if piece == 0:
            part = at(shard, mine_start, cut)
        else:
            part = at(shard, cut, length - cut)
        return remote(
            part,
            part,
            core_send.at[way, s - 1, piece],
            core_recv.at[way, s - 1, piece],
            sibling,
        )

    def corex_copy(way, s, shard):
        part = at(shard, other_start, cut)
        return remote(part, part, corex_send.at[way, s - 1], corex_recv.at[way, s - 1], sibling)

    def shard_of(way, s, c):
        return 2 * chip_at(p - s if way == 0 else p + s) + c

    def pass_on(s, piece):
        for way in range(2) if s < half else (piece,):
            shard = shard_of(way, s, core)
            ring_copy(way, s, piece, shard).wait_recv()
            if s + 1 < half or (s + 1 == half and way == piece):
                go(ring_copy(way, s + 1, piece, shard))
            slot = way if s < half else 0
            if piece == 0:
                go(x_copy(slot, s, shard, mine_start))
            go(core_copy(slot, s, piece, shard))

    def finish(s):
        for way in range(2 if s < half else 1):
            shard = shard_of(way, s, core)
            x_copy(way, s, shard, other_start).wait_recv()
            go(corex_copy(way, s, shard))

    def collect(s):
        for way in range(2 if s < half else 1):
            shard = shard_of(way, s, 1 - core)
            for piece in range(2):
                core_copy(way, s, piece, shard).wait_recv()
            corex_copy(way, s, shard).wait_recv()

    def store(shard):
        columns = pl.ds(pl.multiple_of(shard * width, LANES), width)
        return pltpu.make_async_copy(ig.at[:, columns], ig_hbm.at[:, columns], ig_sem.at[shard])

    def consume(shard):
        columns = pl.ds(pl.multiple_of(shard * width, LANES), width)
        w = w_all[shard]
        total[...] += jnp.dot(acts[:, columns], w, preferred_element_type=jnp.float32)
        back = lax.dot_general(mg[...], w, LAST, preferred_element_type=jnp.float32)
        back += jnp.dot(
            pulled2[...], share_in1[shard, :, :width], preferred_element_type=jnp.float32
        )
        ig[:, columns] = back.astype(jnp.bfloat16)
        store(shard).start()

    def compute(s):
        if s > 0:
            collect(s)
        count = 4 if 0 < s < half else 2

        @pl.loop(0, count)
        def _(t):
            sign = 2 * lax.div(t, 2) - 1
            consume(2 * chip_at(p + s * sign) + lax.rem(t, 2))

    share_start(0)
    load.wait()
    for piece in range(2):
        for way in range(2):
            go(ring_copy(way, 1, piece, f))
    own = remote(w_all.at[f], w_all.at[f], own_send, own_recv, sibling)
    go(own)

    live = (tenant[...] >= 0).astype(jnp.float32)
    size = live.shape[1]
    diagonal = lax.broadcasted_iota(jnp.int32, (size, size), 0) == lax.broadcasted_iota(
        jnp.int32, (size, size), 1
    )
    live_col[...] = jnp.sum(
        jnp.where(diagonal, jnp.broadcast_to(live, (size, size)), 0.0), axis=1, keepdims=True
    )
    mg[...] = (grad[...].astype(jnp.float32) * live_col[...]).astype(jnp.bfloat16)
    tenants = table.shape[0]

    @pl.loop(0, n)
    def _(b):
        tenant_of = lax.fori_loop(
            0,
            tenants,
            lambda t, count: count + (offsets[t + 1] <= b * BLOCK).astype(jnp.int32),
            jnp.int32(0),
        )
        slots[b] = table[jnp.minimum(tenant_of, tenants - 1)]

    pass_on(1, 0)
    pass_on(1, 1)
    share_wait(0)

    @pl.loop(0, n)
    def _(b):
        share_out[1, b] = share_in0[slots[b]]

    share_start(1)
    pass_on(2, 0)
    pass_on(2, 1)
    share_wait(1)

    fetch.wait()
    rank = down.shape[1]
    shrunk = jnp.zeros((rank, size), jnp.float32)
    pulled = jnp.zeros((rank, size), jnp.float32)
    for j in range(n):
        shrunk += lax.dot_general(
            share_in1[j, :, :width],
            acts[:, j * width : (j + 1) * width],
            LAST,
            preferred_element_type=jnp.float32,
        )
    for k in range(ups):
        pulled += lax.dot_general(
            share_in1[k, :, width:],
            mg[:, k * LANES : (k + 1) * LANES],
            LAST,
            preferred_element_type=jnp.float32,
        )
    scale = adapter_scale_factor
    shrunk2_f32 = shrunk.astype(jnp.bfloat16).astype(jnp.float32) * scale
    pulled2_f32 = pulled.astype(jnp.bfloat16).astype(jnp.float32) * scale
    shrunk2_t = shrunk2_f32.astype(jnp.bfloat16)
    pulled2_t = pulled2_f32.astype(jnp.bfloat16)
    shrunk2 = shrunk2_f32.T.astype(jnp.bfloat16)
    pulled2[...] = pulled2_f32.T.astype(jnp.bfloat16)
    for j in range(n):
        share_out[2, j, :, :width] = jnp.dot(
            pulled2_t, acts[:, j * width : (j + 1) * width], preferred_element_type=jnp.float32
        ).astype(jnp.bfloat16)
    for k in range(ups):
        columns = slice(k * LANES, (k + 1) * LANES)
        term = jnp.dot(shrunk2_t, mg[:, columns], preferred_element_type=jnp.float32).astype(
            jnp.bfloat16
        )
        for j in range(k, n, ups):
            share_out[2, j, :, width:] = term
        total[:, columns] = jnp.dot(
            shrunk2, share_in1[k, :, width:], preferred_element_type=jnp.float32
        )
    share_start(2)
    remote(
        w_all.at[2 * chip + 1 - core], w_all.at[2 * chip + 1 - core], own_send, own_recv, sibling
    ).wait_recv()
    compute(0)
    finish(1)
    compute(1)
    pass_on(3, 0)
    pass_on(3, 1)
    share_wait(2)

    @pl.loop(0, n)
    def _(slot):
        summed = jnp.zeros(share_in2.shape[1:], jnp.float32)
        for b in range(n):
            summed += jnp.where(slots[b] == slot, share_in2[b].astype(jnp.float32), 0.0)
        share_out[3, slot] = summed.astype(jnp.bfloat16)

    share_start(3)
    finish(2)
    compute(2)
    for s in range(3, half):
        pass_on(s + 1, 0)
        pass_on(s + 1, 1)
        finish(s)
        compute(s)
    finish(half)
    share_wait(3)
    for j in range(n):
        down_grad[0, :, j * width : (j + 1) * width] = share_in3[j, :, :width].astype(jnp.float32)
    for k in range(ups):
        up_grad[0, :, k * LANES : (k + 1) * LANES] = share_in3[k, :, width:].astype(jnp.float32)
    compute(half)
    out[...] = (total[...] * live_col[...]).astype(jnp.bfloat16)
    @pl.loop(0, n)
    def _(shard):
        store(shard).wait()

    for copy in sends:
        copy.wait_send()
    for phase in range(4):

        @pl.loop(1, n)
        def _(d):
            share_copy(phase, lax.rem(f + d, n), f).wait_send()


def fused(
    activations,
    grad_out,
    token_tenant,
    segment_offsets,
    value_weight,
    down_weight_pool,
    up_weight_pool,
    page_table,
):
    n = lax.axis_size("fsdp")
    tokens, model = activations.shape
    rows, out_width = value_weight.shape
    rank = down_weight_pool.shape[1]
    steps = n // 4
    vmem = pl.BlockSpec(memory_space=pltpu.VMEM)
    hbm = pl.BlockSpec(memory_space=pl.ANY)
    smem = pl.BlockSpec(memory_space=pltpu.SMEM)
    dma = pltpu.SemaphoreType.DMA
    return pl.pallas_call(
        functools.partial(fused_kernel, n),
        out_shape=(
            jax.ShapeDtypeStruct((tokens, out_width), jnp.bfloat16),
            jax.ShapeDtypeStruct((tokens, model), jnp.bfloat16),
            jax.ShapeDtypeStruct((1, rank, model), jnp.float32),
            jax.ShapeDtypeStruct((1, rank, out_width), jnp.float32),
        ),
        in_specs=[hbm, vmem, vmem, smem, smem, hbm, vmem, vmem],
        out_specs=[vmem, hbm, vmem, vmem],
        scratch_shapes=[
            pltpu.VMEM((n, rows, out_width), jnp.bfloat16),
            pltpu.VMEM((tokens, out_width), jnp.bfloat16),
            pltpu.VMEM((tokens, out_width), jnp.float32),
            pltpu.VMEM((4, n, rank, model // n + LANES), jnp.bfloat16),
            pltpu.VMEM((n, rank, model // n + LANES), jnp.bfloat16),
            pltpu.VMEM((n, rank, model // n + LANES), jnp.bfloat16),
            pltpu.VMEM((n, rank, model // n + LANES), jnp.bfloat16),
            pltpu.VMEM((n, rank, model // n + LANES), jnp.bfloat16),
            pltpu.SMEM((n,), jnp.int32),
            pltpu.VMEM((tokens, rank), jnp.bfloat16),
            pltpu.VMEM((tokens, 1), jnp.float32),
            pltpu.VMEM((tokens, model), jnp.bfloat16),
            pltpu.VMEM((tokens, model), jnp.bfloat16),
            dma,
            dma((n,)),
            dma,
        ]
        + [dma((2, steps, 2))] * 2
        + [dma((2, steps))] * 2
        + [dma((2, steps, 2))] * 2
        + [dma((2, steps))] * 2
        + [dma, dma, dma((4, n)), dma((4, n))],
        compiler_params=pltpu.CompilerParams(
            collective_id=0, has_side_effects=True, vmem_limit_bytes=56 * 2**20
        ),
        cost_estimate=pl.CostEstimate(
            flops=4 * tokens * model * out_width,
            bytes_accessed=4 * tokens * model + 4 * model * out_width // n,
            transcendentals=0,
        ),
    )(
        activations,
        grad_out,
        token_tenant.reshape(1, tokens),
        segment_offsets,
        page_table,
        value_weight,
        down_weight_pool,
        up_weight_pool,
    )


def either(*args):
    n = lax.axis_size("fsdp")
    tokens, model = args[0].shape
    rows, out_width = args[4].shape
    slots, rank = args[5].shape[:2]
    fits = (
        lax.axis_size("groups") == 2
        and n % 8 == 0
        and n <= 32
        and tokens == BLOCK
        and slots == 1
        and rank % 16 == 0
        and model % (n * LANES) == 0
        and out_width % LANES == 0
        and out_width // LANES <= n
        and rows >= 128
        and rows % 16 == 0
    )
    return (fused if fits else on_device)(*args)


def solution(mesh):
    placed = (
        P(("groups", "fsdp"), None),
        P(("groups", "fsdp"), None),
        P(("groups", "fsdp")),
        P("groups"),
        P("fsdp", None),
        P("fsdp", None, None),
        P("fsdp", None, None),
        P(),
    )
    return jax.shard_map(
        either,
        mesh=mesh,
        in_specs=placed,
        out_specs=(
            P(("groups", "fsdp"), None),
            P(("groups", "fsdp"), None),
            P(("groups", "fsdp"), None, None),
            P(("groups", "fsdp"), None, None),
        ),
        check_vma=False,
    )
```

```python
import functools

import jax
import jax.numpy as jnp
from jax import lax
from jax.experimental import pallas as pl
from jax.experimental.pallas import tpu as pltpu
from jax.sharding import PartitionSpec as P

BLOCK = 128


adapter_scale_factor = 2.0


def on_device(
    activations,
    grad_out,
    token_tenant,
    segment_offsets,
    value_weight,
    down_weight_pool,
    up_weight_pool,
    page_table,
):
    devices = lax.axis_size("fsdp")
    tok_rows, hidden_model_width = activations.shape
    output_width = grad_out.shape[1]
    local_slot_count = down_weight_pool.shape[0]
    adapter_rank_size = down_weight_pool.shape[1]
    tenants = page_table.shape[0]
    local_block_count = tok_rows // BLOCK
    blocks_all = local_block_count * devices
    active_token_rows = token_tenant >= 0
    masked_grad = grad_out * active_token_rows.astype(jnp.bfloat16)[:, None]
    contract_last = (((1,), (1,)), ((), ()))
    full_weight = lax.all_gather(value_weight, "fsdp", axis=0, tiled=True)
    base_output_rows = jnp.dot(activations, full_weight, preferred_element_type=jnp.float32)
    base_gradient_input = lax.dot_general(
        masked_grad, full_weight, contract_last, preferred_element_type=jnp.float32
    )
    flattened_down_weight = down_weight_pool.reshape(
        local_slot_count, adapter_rank_size * hidden_model_width
    )
    flattened_up_weight = up_weight_pool.reshape(local_slot_count, adapter_rank_size * output_width)
    held_down, held_up = (
        lax.all_to_all(flattened_down_weight, "fsdp", split_axis=1, concat_axis=0, tiled=True),
        lax.all_to_all(flattened_up_weight, "fsdp", split_axis=1, concat_axis=0, tiled=True),
    )
    share_down = held_down.shape[1]
    share_up = held_up.shape[1]
    block_first = lax.iota(jnp.int32, blocks_all) * BLOCK
    block_tenant = jnp.sum(
        (segment_offsets[1:][None, :] <= block_first[:, None]).astype(jnp.int32), axis=1
    )
    tenant_match = block_tenant[:, None] == lax.iota(jnp.int32, tenants)[None, :]
    block_slot = jnp.sum(jnp.where(tenant_match, page_table[None, :], 0), axis=1)
    send_down = jnp.take(held_down, block_slot, axis=0).reshape(
        devices, local_block_count, share_down
    )
    send_up = jnp.take(held_up, block_slot, axis=0).reshape(devices, local_block_count, share_up)
    fetched_down_weight, fetched_up_weight = (
        lax.all_to_all(send_down, "fsdp", split_axis=0, concat_axis=2, tiled=True),
        lax.all_to_all(send_up, "fsdp", split_axis=0, concat_axis=2, tiled=True),
    )
    down_weight_block = fetched_down_weight.reshape(
        local_block_count, adapter_rank_size, hidden_model_width
    )
    up_weight_block = fetched_up_weight.reshape(local_block_count, adapter_rank_size, output_width)
    input_blocks = activations.reshape(local_block_count, BLOCK, hidden_model_width)
    gradient_blocks = masked_grad.reshape(local_block_count, BLOCK, output_width)
    reduced_rank_rows = jnp.einsum(
        "bnd,brd->bnr", input_blocks, down_weight_block, preferred_element_type=jnp.float32
    ).astype(jnp.bfloat16)
    expanded_rows = jnp.einsum(
        "bnr,bro->bno", reduced_rank_rows, up_weight_block, preferred_element_type=jnp.float32
    ).reshape(tok_rows, output_width)
    pulled_rows = jnp.einsum(
        "bno,bro->bnr", gradient_blocks, up_weight_block, preferred_element_type=jnp.float32
    ).astype(jnp.bfloat16)
    scattered_gradient = jnp.einsum(
        "bnr,brd->bnd", pulled_rows, down_weight_block, preferred_element_type=jnp.float32
    ).reshape(tok_rows, hidden_model_width)
    adapted_value_output = (
        (base_output_rows + adapter_scale_factor * expanded_rows)
        * active_token_rows.astype(jnp.float32)[:, None]
    ).astype(jnp.bfloat16)
    input_gradient = (base_gradient_input + adapter_scale_factor * scattered_gradient).astype(
        jnp.bfloat16
    )
    down_weight_terms = adapter_scale_factor * jnp.einsum(
        "kpz,kpj->kzj", pulled_rows, input_blocks, preferred_element_type=jnp.float32
    )
    up_weight_terms = adapter_scale_factor * jnp.einsum(
        "yig,yiw->ygw", reduced_rank_rows, gradient_blocks, preferred_element_type=jnp.float32
    )
    ret_down = down_weight_terms.reshape(local_block_count, devices, share_down)
    ret_up = up_weight_terms.reshape(local_block_count, devices, share_up)
    back_down, back_up = (
        lax.all_to_all(ret_down, "fsdp", split_axis=1, concat_axis=0, tiled=True),
        lax.all_to_all(ret_up, "fsdp", split_axis=1, concat_axis=0, tiled=True),
    )
    recv_down = back_down.reshape(blocks_all, share_down)
    recv_up = back_up.reshape(blocks_all, share_up)
    slot_match = (block_slot[None, :] == lax.iota(jnp.int32, tenants)[:, None]).astype(jnp.float32)
    sum_down = jnp.dot(
        slot_match, recv_down, precision=lax.Precision.HIGHEST, preferred_element_type=jnp.float32
    )
    sum_up = jnp.dot(
        slot_match, recv_up, precision=lax.Precision.HIGHEST, preferred_element_type=jnp.float32
    )
    resident_down_weight, resident_up_weight = (
        lax.all_to_all(sum_down, "fsdp", split_axis=0, concat_axis=1, tiled=True),
        lax.all_to_all(sum_up, "fsdp", split_axis=0, concat_axis=1, tiled=True),
    )
    down_pool_gradient = resident_down_weight.reshape(
        local_slot_count, adapter_rank_size, hidden_model_width
    )
    up_pool_gradient = resident_up_weight.reshape(local_slot_count, adapter_rank_size, output_width)
    return (adapted_value_output, input_gradient, down_pool_gradient, up_pool_gradient)


LAST = (((1,), (1,)), ((), ()))
FIRST = (((0,), (0,)), ((), ()))
LANES = 128


def remote(src, dst, send, recv, where):
    return pltpu.make_async_remote_copy(
        src_ref=src,
        dst_ref=dst,
        send_sem=send,
        recv_sem=recv,
        device_id=where,
        device_id_type=pl.DeviceIdType.MESH,
    )


def fused_kernel(
    n,
    acts_hbm,
    grad,
    tenant,
    offsets,
    table,
    w_hbm,
    down,
    up,
    out,
    ig_hbm,
    down_grad,
    up_grad,
    w_all,
    mg,
    total,
    share_out,
    share_in0,
    share_in1,
    share_in2,
    share_in3,
    slots,
    pulled2,
    live_col,
    acts,
    ig,
    acts_sem,
    ig_sem,
    local_sem,
    ring_send,
    ring_recv,
    x_send,
    x_recv,
    core_send,
    core_recv,
    corex_send,
    corex_recv,
    own_send,
    own_recv,
    share_send,
    share_recv,
):
    share_in = (share_in0, share_in1, share_in2, share_in3)
    x = lax.axis_index("groups")
    f = lax.axis_index("fsdp")
    m = n // 2
    half = m // 2
    chip, core = lax.div(f, 2), lax.rem(f, 2)
    z, y = lax.div(chip, 2), lax.rem(chip, 2)
    p = z + y * (m - 1 - 2 * z)
    width = down.shape[2] // n
    out_width = up.shape[2]
    ups = out_width // LANES
    rows = w_all.shape[1]
    cut = ((rows * 208) // 512) // 16 * 16
    length = rows - cut

    def chip_at(position):
        q = lax.rem(position + 2 * m, m)
        y_q = lax.div(q, half)
        return 2 * (q + y_q * (m - 1 - 2 * q)) + y_q

    def at(shard, start, size):
        return w_all.at[shard, pl.ds(pl.multiple_of(start, 16), size), :]

    right = {"fsdp": 2 * chip_at(p + 1) + core}
    left = {"fsdp": 2 * chip_at(p - 1) + core}
    sibling = {"fsdp": 2 * chip + 1 - core}
    across = {"groups": 1 - x}
    mine_start = x * length
    other_start = (1 - x) * length

    barrier = pltpu.get_barrier_semaphore()

    @pl.loop(1, n)
    def _(d):
        pl.semaphore_signal(
            barrier,
            inc=1,
            device_id={"fsdp": lax.rem(f + d, n)},
            device_id_type=pl.DeviceIdType.MESH,
        )

    pl.semaphore_signal(barrier, inc=1, device_id=across, device_id_type=pl.DeviceIdType.MESH)
    fetch = pltpu.make_async_copy(acts_hbm, acts, acts_sem)
    load = pltpu.make_async_copy(w_hbm, w_all.at[f], local_sem)
    load.start()
    fetch.start()
    for j in range(n):
        share_out[0, j, :, :width] = down[0, :, j * width : (j + 1) * width]
        k = j % ups
        share_out[0, j, :, width:] = up[0, :, k * LANES : (k + 1) * LANES]
    pl.semaphore_wait(barrier, n)

    def share_copy(phase, j, slot):
        return remote(
            share_out.at[phase, j],
            share_in[phase].at[slot],
            share_send.at[phase, j],
            share_recv.at[phase, slot],
            {"fsdp": j},
        )

    def share_start(phase):
        @pl.loop(1, n)
        def _(d):
            j = lax.rem(f + d, n)
            share_copy(phase, j, f).start()

        share_in[phase][f] = share_out[phase, f]

    def share_wait(phase):
        @pl.loop(1, n)
        def _(d):
            j = lax.rem(f + d, n)
            share_copy(phase, j, j).wait_recv()

    sends = []

    def go(copy):
        copy.start()
        sends.append(copy)

    def ring_copy(way, s, piece, shard):
        if piece == 0:
            part = at(shard, mine_start, cut)
        else:
            part = at(shard, cut, length - cut)
        return remote(
            part,
            part,
            ring_send.at[way, s - 1, piece],
            ring_recv.at[way, s - 1, piece],
            (right, left)[way],
        )

    def x_copy(way, s, shard, start):
        part = at(shard, start, cut)
        return remote(part, part, x_send.at[way, s - 1], x_recv.at[way, s - 1], across)

    def core_copy(way, s, piece, shard):
        if piece == 0:
            part = at(shard, mine_start, cut)
        else:
            part = at(shard, cut, length - cut)
        return remote(
            part,
            part,
            core_send.at[way, s - 1, piece],
            core_recv.at[way, s - 1, piece],
            sibling,
        )

    def corex_copy(way, s, shard):
        part = at(shard, other_start, cut)
        return remote(part, part, corex_send.at[way, s - 1], corex_recv.at[way, s - 1], sibling)

    def shard_of(way, s, c):
        return 2 * chip_at(p - s if way == 0 else p + s) + c

    def pass_on(s, piece):
        for way in range(2) if s < half else (piece,):
            shard = shard_of(way, s, core)
            ring_copy(way, s, piece, shard).wait_recv()
            slot = way if s < half else 0
            if piece == 0:
                go(x_copy(slot, s, shard, mine_start))
            if s + 1 < half or (s + 1 == half and way == piece):
                go(ring_copy(way, s + 1, piece, shard))
            go(core_copy(slot, s, piece, shard))

    def finish(s):
        for way in range(2 if s < half else 1):
            shard = shard_of(way, s, core)
            x_copy(way, s, shard, other_start).wait_recv()
            go(corex_copy(way, s, shard))

    def collect(s):
        for way in range(2 if s < half else 1):
            shard = shard_of(way, s, 1 - core)
            for piece in range(2):
                core_copy(way, s, piece, shard).wait_recv()
            corex_copy(way, s, shard).wait_recv()

    def store(shard):
        columns = pl.ds(pl.multiple_of(shard * width, LANES), width)
        return pltpu.make_async_copy(ig.at[:, columns], ig_hbm.at[:, columns], ig_sem.at[shard])

    def consume(shard):
        columns = pl.ds(pl.multiple_of(shard * width, LANES), width)
        w = w_all[shard]
        total[...] += jnp.dot(acts[:, columns], w, preferred_element_type=jnp.float32)
        back = lax.dot_general(mg[...], w, LAST, preferred_element_type=jnp.float32)
        back += jnp.dot(
            pulled2[...], share_in1[shard, :, :width], preferred_element_type=jnp.float32
        )
        ig[:, columns] = back.astype(jnp.bfloat16)
        store(shard).start()

    def compute(s):
        if s > 0:
            collect(s)
        count = 4 if 0 < s < half else 2

        @pl.loop(0, count)
        def _(t):
            sign = 2 * lax.div(t, 2) - 1
            consume(2 * chip_at(p + s * sign) + lax.rem(t, 2))

    share_start(0)
    load.wait()
    for piece in range(2):
        for way in range(2):
            go(ring_copy(way, 1, piece, f))
    own = remote(w_all.at[f], w_all.at[f], own_send, own_recv, sibling)
    go(own)

    live = (tenant[...] >= 0).astype(jnp.float32)
    size = live.shape[1]
    diagonal = lax.broadcasted_iota(jnp.int32, (size, size), 0) == lax.broadcasted_iota(
        jnp.int32, (size, size), 1
    )
    live_col[...] = jnp.sum(
        jnp.where(diagonal, jnp.broadcast_to(live, (size, size)), 0.0), axis=1, keepdims=True
    )
    mg[...] = (grad[...].astype(jnp.float32) * live_col[...]).astype(jnp.bfloat16)
    tenants = table.shape[0]

    @pl.loop(0, n)
    def _(b):
        tenant_of = lax.fori_loop(
            0,
            tenants,
            lambda t, count: count + (offsets[t + 1] <= b * BLOCK).astype(jnp.int32),
            jnp.int32(0),
        )
        slots[b] = table[jnp.minimum(tenant_of, tenants - 1)]

    pass_on(1, 0)
    pass_on(1, 1)
    share_wait(0)

    @pl.loop(0, n)
    def _(b):
        share_out[1, b] = share_in0[slots[b]]

    share_start(1)
    pass_on(2, 0)
    pass_on(2, 1)
    share_wait(1)

    fetch.wait()
    rank = down.shape[1]
    shrunk = jnp.zeros((rank, size), jnp.float32)
    pulled = jnp.zeros((rank, size), jnp.float32)
    for j in range(n):
        shrunk += lax.dot_general(
            share_in1[j, :, :width],
            acts[:, j * width : (j + 1) * width],
            LAST,
            preferred_element_type=jnp.float32,
        )
    for k in range(ups):
        pulled += lax.dot_general(
            share_in1[k, :, width:],
            mg[:, k * LANES : (k + 1) * LANES],
            LAST,
            preferred_element_type=jnp.float32,
        )
    scale = adapter_scale_factor
    shrunk2_f32 = shrunk.astype(jnp.bfloat16).astype(jnp.float32) * scale
    pulled2_f32 = pulled.astype(jnp.bfloat16).astype(jnp.float32) * scale
    shrunk2_t = shrunk2_f32.astype(jnp.bfloat16)
    pulled2_t = pulled2_f32.astype(jnp.bfloat16)
    shrunk2 = shrunk2_f32.T.astype(jnp.bfloat16)
    pulled2[...] = pulled2_f32.T.astype(jnp.bfloat16)
    for j in range(n):
        share_out[2, j, :, :width] = jnp.dot(
            pulled2_t, acts[:, j * width : (j + 1) * width], preferred_element_type=jnp.float32
        ).astype(jnp.bfloat16)
    for k in range(ups):
        columns = slice(k * LANES, (k + 1) * LANES)
        term = jnp.dot(shrunk2_t, mg[:, columns], preferred_element_type=jnp.float32).astype(
            jnp.bfloat16
        )
        for j in range(k, n, ups):
            share_out[2, j, :, width:] = term
        total[:, columns] = jnp.dot(
            shrunk2, share_in1[k, :, width:], preferred_element_type=jnp.float32
        )
    share_start(2)
    remote(
        w_all.at[2 * chip + 1 - core], w_all.at[2 * chip + 1 - core], own_send, own_recv, sibling
    ).wait_recv()
    compute(0)
    finish(1)
    compute(1)
    pass_on(3, 0)
    pass_on(3, 1)
    share_wait(2)

    @pl.loop(0, n)
    def _(slot):
        summed = jnp.zeros(share_in2.shape[1:], jnp.float32)
        for b in range(n):
            summed += jnp.where(slots[b] == slot, share_in2[b].astype(jnp.float32), 0.0)
        share_out[3, slot] = summed.astype(jnp.bfloat16)

    share_start(3)
    finish(2)
    compute(2)
    for s in range(3, half):
        pass_on(s + 1, 0)
        pass_on(s + 1, 1)
        finish(s)
        compute(s)
    finish(half)
    share_wait(3)
    for j in range(n):
        down_grad[0, :, j * width : (j + 1) * width] = share_in3[j, :, :width].astype(jnp.float32)
    for k in range(ups):
        up_grad[0, :, k * LANES : (k + 1) * LANES] = share_in3[k, :, width:].astype(jnp.float32)
    compute(half)
    out[...] = (total[...] * live_col[...]).astype(jnp.bfloat16)
    @pl.loop(0, n)
    def _(shard):
        store(shard).wait()

    for copy in sends:
        copy.wait_send()
    for phase in range(4):

        @pl.loop(1, n)
        def _(d):
            share_copy(phase, lax.rem(f + d, n), f).wait_send()


def fused(
    activations,
    grad_out,
    token_tenant,
    segment_offsets,
    value_weight,
    down_weight_pool,
    up_weight_pool,
    page_table,
):
    n = lax.axis_size("fsdp")
    tokens, model = activations.shape
    rows, out_width = value_weight.shape
    rank = down_weight_pool.shape[1]
    steps = n // 4
    vmem = pl.BlockSpec(memory_space=pltpu.VMEM)
    hbm = pl.BlockSpec(memory_space=pl.ANY)
    smem = pl.BlockSpec(memory_space=pltpu.SMEM)
    dma = pltpu.SemaphoreType.DMA
    return pl.pallas_call(
        functools.partial(fused_kernel, n),
        out_shape=(
            jax.ShapeDtypeStruct((tokens, out_width), jnp.bfloat16),
            jax.ShapeDtypeStruct((tokens, model), jnp.bfloat16),
            jax.ShapeDtypeStruct((1, rank, model), jnp.float32),
            jax.ShapeDtypeStruct((1, rank, out_width), jnp.float32),
        ),
        in_specs=[hbm, vmem, vmem, smem, smem, hbm, vmem, vmem],
        out_specs=[vmem, hbm, vmem, vmem],
        scratch_shapes=[
            pltpu.VMEM((n, rows, out_width), jnp.bfloat16),
            pltpu.VMEM((tokens, out_width), jnp.bfloat16),
            pltpu.VMEM((tokens, out_width), jnp.float32),
            pltpu.VMEM((4, n, rank, model // n + LANES), jnp.bfloat16),
            pltpu.VMEM((n, rank, model // n + LANES), jnp.bfloat16),
            pltpu.VMEM((n, rank, model // n + LANES), jnp.bfloat16),
            pltpu.VMEM((n, rank, model // n + LANES), jnp.bfloat16),
            pltpu.VMEM((n, rank, model // n + LANES), jnp.bfloat16),
            pltpu.SMEM((n,), jnp.int32),
            pltpu.VMEM((tokens, rank), jnp.bfloat16),
            pltpu.VMEM((tokens, 1), jnp.float32),
            pltpu.VMEM((tokens, model), jnp.bfloat16),
            pltpu.VMEM((tokens, model), jnp.bfloat16),
            dma,
            dma((n,)),
            dma,
        ]
        + [dma((2, steps, 2))] * 2
        + [dma((2, steps))] * 2
        + [dma((2, steps, 2))] * 2
        + [dma((2, steps))] * 2
        + [dma, dma, dma((4, n)), dma((4, n))],
        compiler_params=pltpu.CompilerParams(
            collective_id=0, has_side_effects=True, vmem_limit_bytes=56 * 2**20
        ),
        cost_estimate=pl.CostEstimate(
            flops=4 * tokens * model * out_width,
            bytes_accessed=4 * tokens * model + 4 * model * out_width // n,
            transcendentals=0,
        ),
    )(
        activations,
        grad_out,
        token_tenant.reshape(1, tokens),
        segment_offsets,
        page_table,
        value_weight,
        down_weight_pool,
        up_weight_pool,
    )


def either(*args):
    n = lax.axis_size("fsdp")
    tokens, model = args[0].shape
    rows, out_width = args[4].shape
    slots, rank = args[5].shape[:2]
    fits = (
        lax.axis_size("groups") == 2
        and n % 8 == 0
        and n <= 32
        and tokens == BLOCK
        and slots == 1
        and rank % 16 == 0
        and model % (n * LANES) == 0
        and out_width % LANES == 0
        and out_width // LANES <= n
        and rows >= 128
        and rows % 16 == 0
    )
    return (fused if fits else on_device)(*args)


def solution(mesh):
    placed = (
        P(("groups", "fsdp"), None),
        P(("groups", "fsdp"), None),
        P(("groups", "fsdp")),
        P("groups"),
        P("fsdp", None),
        P("fsdp", None, None),
        P("fsdp", None, None),
        P(),
    )
    return jax.shard_map(
        either,
        mesh=mesh,
        in_specs=placed,
        out_specs=(
            P(("groups", "fsdp"), None),
            P(("groups", "fsdp"), None),
            P(("groups", "fsdp"), None, None),
            P(("groups", "fsdp"), None, None),
        ),
        check_vma=False,
    )
```

```python
import functools

import jax
import jax.numpy as jnp
from jax import lax
from jax.experimental import pallas as pl
from jax.experimental.pallas import tpu as pltpu
from jax.sharding import PartitionSpec as P

BLOCK = 128


adapter_scale_factor = 2.0


def on_device(
    activations,
    grad_out,
    token_tenant,
    segment_offsets,
    value_weight,
    down_weight_pool,
    up_weight_pool,
    page_table,
):
    devices = lax.axis_size("fsdp")
    tok_rows, hidden_model_width = activations.shape
    output_width = grad_out.shape[1]
    local_slot_count = down_weight_pool.shape[0]
    adapter_rank_size = down_weight_pool.shape[1]
    tenants = page_table.shape[0]
    local_block_count = tok_rows // BLOCK
    blocks_all = local_block_count * devices
    active_token_rows = token_tenant >= 0
    masked_grad = grad_out * active_token_rows.astype(jnp.bfloat16)[:, None]
    contract_last = (((1,), (1,)), ((), ()))
    full_weight = lax.all_gather(value_weight, "fsdp", axis=0, tiled=True)
    base_output_rows = jnp.dot(activations, full_weight, preferred_element_type=jnp.float32)
    base_gradient_input = lax.dot_general(
        masked_grad, full_weight, contract_last, preferred_element_type=jnp.float32
    )
    flattened_down_weight = down_weight_pool.reshape(
        local_slot_count, adapter_rank_size * hidden_model_width
    )
    flattened_up_weight = up_weight_pool.reshape(local_slot_count, adapter_rank_size * output_width)
    held_down, held_up = (
        lax.all_to_all(flattened_down_weight, "fsdp", split_axis=1, concat_axis=0, tiled=True),
        lax.all_to_all(flattened_up_weight, "fsdp", split_axis=1, concat_axis=0, tiled=True),
    )
    share_down = held_down.shape[1]
    share_up = held_up.shape[1]
    block_first = lax.iota(jnp.int32, blocks_all) * BLOCK
    block_tenant = jnp.sum(
        (segment_offsets[1:][None, :] <= block_first[:, None]).astype(jnp.int32), axis=1
    )
    tenant_match = block_tenant[:, None] == lax.iota(jnp.int32, tenants)[None, :]
    block_slot = jnp.sum(jnp.where(tenant_match, page_table[None, :], 0), axis=1)
    send_down = jnp.take(held_down, block_slot, axis=0).reshape(
        devices, local_block_count, share_down
    )
    send_up = jnp.take(held_up, block_slot, axis=0).reshape(devices, local_block_count, share_up)
    fetched_down_weight, fetched_up_weight = (
        lax.all_to_all(send_down, "fsdp", split_axis=0, concat_axis=2, tiled=True),
        lax.all_to_all(send_up, "fsdp", split_axis=0, concat_axis=2, tiled=True),
    )
    down_weight_block = fetched_down_weight.reshape(
        local_block_count, adapter_rank_size, hidden_model_width
    )
    up_weight_block = fetched_up_weight.reshape(local_block_count, adapter_rank_size, output_width)
    input_blocks = activations.reshape(local_block_count, BLOCK, hidden_model_width)
    gradient_blocks = masked_grad.reshape(local_block_count, BLOCK, output_width)
    reduced_rank_rows = jnp.einsum(
        "bnd,brd->bnr", input_blocks, down_weight_block, preferred_element_type=jnp.float32
    ).astype(jnp.bfloat16)
    expanded_rows = jnp.einsum(
        "bnr,bro->bno", reduced_rank_rows, up_weight_block, preferred_element_type=jnp.float32
    ).reshape(tok_rows, output_width)
    pulled_rows = jnp.einsum(
        "bno,bro->bnr", gradient_blocks, up_weight_block, preferred_element_type=jnp.float32
    ).astype(jnp.bfloat16)
    scattered_gradient = jnp.einsum(
        "bnr,brd->bnd", pulled_rows, down_weight_block, preferred_element_type=jnp.float32
    ).reshape(tok_rows, hidden_model_width)
    adapted_value_output = (
        (base_output_rows + adapter_scale_factor * expanded_rows)
        * active_token_rows.astype(jnp.float32)[:, None]
    ).astype(jnp.bfloat16)
    input_gradient = (base_gradient_input + adapter_scale_factor * scattered_gradient).astype(
        jnp.bfloat16
    )
    down_weight_terms = adapter_scale_factor * jnp.einsum(
        "kpz,kpj->kzj", pulled_rows, input_blocks, preferred_element_type=jnp.float32
    )
    up_weight_terms = adapter_scale_factor * jnp.einsum(
        "yig,yiw->ygw", reduced_rank_rows, gradient_blocks, preferred_element_type=jnp.float32
    )
    ret_down = down_weight_terms.reshape(local_block_count, devices, share_down)
    ret_up = up_weight_terms.reshape(local_block_count, devices, share_up)
    back_down, back_up = (
        lax.all_to_all(ret_down, "fsdp", split_axis=1, concat_axis=0, tiled=True),
        lax.all_to_all(ret_up, "fsdp", split_axis=1, concat_axis=0, tiled=True),
    )
    recv_down = back_down.reshape(blocks_all, share_down)
    recv_up = back_up.reshape(blocks_all, share_up)
    slot_match = (block_slot[None, :] == lax.iota(jnp.int32, tenants)[:, None]).astype(jnp.float32)
    sum_down = jnp.dot(
        slot_match, recv_down, precision=lax.Precision.HIGHEST, preferred_element_type=jnp.float32
    )
    sum_up = jnp.dot(
        slot_match, recv_up, precision=lax.Precision.HIGHEST, preferred_element_type=jnp.float32
    )
    resident_down_weight, resident_up_weight = (
        lax.all_to_all(sum_down, "fsdp", split_axis=0, concat_axis=1, tiled=True),
        lax.all_to_all(sum_up, "fsdp", split_axis=0, concat_axis=1, tiled=True),
    )
    down_pool_gradient = resident_down_weight.reshape(
        local_slot_count, adapter_rank_size, hidden_model_width
    )
    up_pool_gradient = resident_up_weight.reshape(local_slot_count, adapter_rank_size, output_width)
    return (adapted_value_output, input_gradient, down_pool_gradient, up_pool_gradient)


LAST = (((1,), (1,)), ((), ()))
FIRST = (((0,), (0,)), ((), ()))
LANES = 128


def remote(src, dst, send, recv, where):
    return pltpu.make_async_remote_copy(
        src_ref=src,
        dst_ref=dst,
        send_sem=send,
        recv_sem=recv,
        device_id=where,
        device_id_type=pl.DeviceIdType.MESH,
    )


def fused_kernel(
    n,
    acts_hbm,
    grad,
    tenant,
    offsets,
    table,
    w_hbm,
    down,
    up,
    out,
    ig_hbm,
    down_grad,
    up_grad,
    w_all,
    mg,
    total,
    share_out,
    share_in0,
    share_in1,
    share_in2,
    share_in3,
    slots,
    pulled2,
    live_col,
    acts,
    ig,
    acts_sem,
    ig_sem,
    local_sem,
    ring_send,
    ring_recv,
    x_send,
    x_recv,
    core_send,
    core_recv,
    corex_send,
    corex_recv,
    own_send,
    own_recv,
    share_send,
    share_recv,
):
    share_in = (share_in0, share_in1, share_in2, share_in3)
    x = lax.axis_index("groups")
    f = lax.axis_index("fsdp")
    m = n // 2
    half = m // 2
    chip, core = lax.div(f, 2), lax.rem(f, 2)
    z, y = lax.div(chip, 2), lax.rem(chip, 2)
    p = z + y * (m - 1 - 2 * z)
    width = down.shape[2] // n
    out_width = up.shape[2]
    ups = out_width // LANES
    rows = w_all.shape[1]
    cut = ((rows * 208) // 512) // 16 * 16
    length = rows - cut

    def chip_at(position):
        q = lax.rem(position + 2 * m, m)
        y_q = lax.div(q, half)
        return 2 * (q + y_q * (m - 1 - 2 * q)) + y_q

    def at(shard, start, size):
        return w_all.at[shard, pl.ds(pl.multiple_of(start, 16), size), :]

    right = {"fsdp": 2 * chip_at(p + 1) + core}
    left = {"fsdp": 2 * chip_at(p - 1) + core}
    sibling = {"fsdp": 2 * chip + 1 - core}
    across = {"groups": 1 - x}
    mine_start = x * length
    other_start = (1 - x) * length

    barrier = pltpu.get_barrier_semaphore()

    @pl.loop(1, n)
    def _(d):
        pl.semaphore_signal(
            barrier,
            inc=1,
            device_id={"fsdp": lax.rem(f + d, n)},
            device_id_type=pl.DeviceIdType.MESH,
        )

    pl.semaphore_signal(barrier, inc=1, device_id=across, device_id_type=pl.DeviceIdType.MESH)
    fetch = pltpu.make_async_copy(acts_hbm, acts, acts_sem)
    load = pltpu.make_async_copy(w_hbm, w_all.at[f], local_sem)
    load.start()
    fetch.start()
    for j in range(n):
        share_out[0, j, :, :width] = down[0, :, j * width : (j + 1) * width]
        k = j % ups
        share_out[0, j, :, width:] = up[0, :, k * LANES : (k + 1) * LANES]
    pl.semaphore_wait(barrier, n)

    def share_copy(phase, j, slot, columns):
        return remote(
            share_out.at[phase, j, :, pl.ds(0, columns)],
            share_in[phase].at[slot, :, pl.ds(0, columns)],
            share_send.at[phase, j],
            share_recv.at[phase, slot],
            {"fsdp": j},
        )

    def share_each(phase, j, slot, holder, act):
        @pl.when(holder < ups)
        def _():
            act(share_copy(phase, j, slot, width + LANES))

        @pl.when(holder >= ups)
        def _():
            act(share_copy(phase, j, slot, width))

    def share_start(phase):
        @pl.loop(1, n)
        def _(d):
            j = lax.rem(f + d, n)
            share_each(phase, j, f, (j, f)[phase % 2], lambda copy: copy.start())

        share_in[phase][f] = share_out[phase, f]

    def share_wait(phase):
        @pl.loop(1, n)
        def _(d):
            j = lax.rem(f + d, n)
            share_each(phase, j, j, (f, j)[phase % 2], lambda copy: copy.wait_recv())

    sends = []

    def go(copy):
        copy.start()
        sends.append(copy)

    def ring_copy(way, s, piece, shard):
        if piece == 0:
            part = at(shard, mine_start, cut)
        else:
            part = at(shard, cut, length - cut)
        return remote(
            part,
            part,
            ring_send.at[way, s - 1, piece],
            ring_recv.at[way, s - 1, piece],
            (right, left)[way],
        )

    def x_copy(way, s, shard, start):
        part = at(shard, start, cut)
        return remote(part, part, x_send.at[way, s - 1], x_recv.at[way, s - 1], across)

    def core_copy(way, s, piece, shard):
        if piece == 0:
            part = at(shard, mine_start, cut)
        else:
            part = at(shard, cut, length - cut)
        return remote(
            part,
            part,
            core_send.at[way, s - 1, piece],
            core_recv.at[way, s - 1, piece],
            sibling,
        )

    def corex_copy(way, s, shard):
        part = at(shard, other_start, cut)
        return remote(part, part, corex_send.at[way, s - 1], corex_recv.at[way, s - 1], sibling)

    def shard_of(way, s, c):
        return 2 * chip_at(p - s if way == 0 else p + s) + c

    def pass_on(s, piece):
        for way in range(2) if s < half else (piece,):
            shard = shard_of(way, s, core)
            ring_copy(way, s, piece, shard).wait_recv()
            slot = way if s < half else 0
            if piece == 0:
                go(x_copy(slot, s, shard, mine_start))
            if s + 1 < half or (s + 1 == half and way == piece):
                go(ring_copy(way, s + 1, piece, shard))
            go(core_copy(slot, s, piece, shard))

    def finish(s):
        for way in range(2 if s < half else 1):
            shard = shard_of(way, s, core)
            x_copy(way, s, shard, other_start).wait_recv()
            go(corex_copy(way, s, shard))

    def collect(s):
        for way in range(2 if s < half else 1):
            shard = shard_of(way, s, 1 - core)
            for piece in range(2):
                core_copy(way, s, piece, shard).wait_recv()
            corex_copy(way, s, shard).wait_recv()

    def store(shard):
        columns = pl.ds(pl.multiple_of(shard * width, LANES), width)
        return pltpu.make_async_copy(ig.at[:, columns], ig_hbm.at[:, columns], ig_sem.at[shard])

    def consume(shard):
        columns = pl.ds(pl.multiple_of(shard * width, LANES), width)
        w = w_all[shard]
        total[...] += jnp.dot(acts[:, columns], w, preferred_element_type=jnp.float32)
        back = lax.dot_general(mg[...], w, LAST, preferred_element_type=jnp.float32)
        back += jnp.dot(
            pulled2[...], share_in1[shard, :, :width], preferred_element_type=jnp.float32
        )
        ig[:, columns] = back.astype(jnp.bfloat16)
        store(shard).start()

    def compute(s):
        if s > 0:
            collect(s)
        count = 4 if 0 < s < half else 2

        @pl.loop(0, count)
        def _(t):
            sign = 2 * lax.div(t, 2) - 1
            consume(2 * chip_at(p + s * sign) + lax.rem(t, 2))

    share_start(0)
    load.wait()
    for piece in range(2):
        for way in range(2):
            go(ring_copy(way, 1, piece, f))
    own = remote(w_all.at[f], w_all.at[f], own_send, own_recv, sibling)
    go(own)

    live = (tenant[...] >= 0).astype(jnp.float32)
    size = live.shape[1]
    diagonal = lax.broadcasted_iota(jnp.int32, (size, size), 0) == lax.broadcasted_iota(
        jnp.int32, (size, size), 1
    )
    live_col[...] = jnp.sum(
        jnp.where(diagonal, jnp.broadcast_to(live, (size, size)), 0.0), axis=1, keepdims=True
    )
    mg[...] = (grad[...].astype(jnp.float32) * live_col[...]).astype(jnp.bfloat16)
    tenants = table.shape[0]

    @pl.loop(0, n)
    def _(b):
        tenant_of = lax.fori_loop(
            0,
            tenants,
            lambda t, count: count + (offsets[t + 1] <= b * BLOCK).astype(jnp.int32),
            jnp.int32(0),
        )
        slots[b] = table[jnp.minimum(tenant_of, tenants - 1)]

    pass_on(1, 0)
    pass_on(1, 1)
    share_wait(0)

    @pl.loop(0, n)
    def _(b):
        share_out[1, b] = share_in0[slots[b]]

    share_start(1)
    pass_on(2, 0)
    pass_on(2, 1)
    share_wait(1)

    fetch.wait()
    rank = down.shape[1]
    shrunk = jnp.zeros((rank, size), jnp.float32)
    pulled = jnp.zeros((rank, size), jnp.float32)
    for j in range(n):
        shrunk += lax.dot_general(
            share_in1[j, :, :width],
            acts[:, j * width : (j + 1) * width],
            LAST,
            preferred_element_type=jnp.float32,
        )
    for k in range(ups):
        pulled += lax.dot_general(
            share_in1[k, :, width:],
            mg[:, k * LANES : (k + 1) * LANES],
            LAST,
            preferred_element_type=jnp.float32,
        )
    scale = adapter_scale_factor
    shrunk2_f32 = shrunk.astype(jnp.bfloat16).astype(jnp.float32) * scale
    pulled2_f32 = pulled.astype(jnp.bfloat16).astype(jnp.float32) * scale
    shrunk2_t = shrunk2_f32.astype(jnp.bfloat16)
    pulled2_t = pulled2_f32.astype(jnp.bfloat16)
    shrunk2 = shrunk2_f32.T.astype(jnp.bfloat16)
    pulled2[...] = pulled2_f32.T.astype(jnp.bfloat16)
    for j in range(n):
        share_out[2, j, :, :width] = jnp.dot(
            pulled2_t, acts[:, j * width : (j + 1) * width], preferred_element_type=jnp.float32
        ).astype(jnp.bfloat16)
    for k in range(ups):
        columns = slice(k * LANES, (k + 1) * LANES)
        term = jnp.dot(shrunk2_t, mg[:, columns], preferred_element_type=jnp.float32).astype(
            jnp.bfloat16
        )
        for j in range(k, n, ups):
            share_out[2, j, :, width:] = term
        total[:, columns] = jnp.dot(
            shrunk2, share_in1[k, :, width:], preferred_element_type=jnp.float32
        )
    share_start(2)
    remote(
        w_all.at[2 * chip + 1 - core], w_all.at[2 * chip + 1 - core], own_send, own_recv, sibling
    ).wait_recv()
    compute(0)
    finish(1)
    compute(1)
    pass_on(3, 0)
    pass_on(3, 1)
    share_wait(2)

    @pl.loop(0, n)
    def _(slot):
        summed = jnp.zeros(share_in2.shape[1:], jnp.float32)
        for b in range(n):
            summed += jnp.where(slots[b] == slot, share_in2[b].astype(jnp.float32), 0.0)
        share_out[3, slot] = summed.astype(jnp.bfloat16)

    share_start(3)
    finish(2)
    compute(2)
    for s in range(3, half):
        pass_on(s + 1, 0)
        pass_on(s + 1, 1)
        finish(s)
        compute(s)
    finish(half)
    share_wait(3)
    for j in range(n):
        down_grad[0, :, j * width : (j + 1) * width] = share_in3[j, :, :width].astype(jnp.float32)
    for k in range(ups):
        up_grad[0, :, k * LANES : (k + 1) * LANES] = share_in3[k, :, width:].astype(jnp.float32)
    compute(half)
    out[...] = (total[...] * live_col[...]).astype(jnp.bfloat16)
    @pl.loop(0, n)
    def _(shard):
        store(shard).wait()

    for copy in sends:
        copy.wait_send()
    for phase in range(4):

        @pl.loop(1, n)
        def _(d):
            j = lax.rem(f + d, n)
            share_each(phase, j, f, (j, f)[phase % 2], lambda copy: copy.wait_send())


def fused(
    activations,
    grad_out,
    token_tenant,
    segment_offsets,
    value_weight,
    down_weight_pool,
    up_weight_pool,
    page_table,
):
    n = lax.axis_size("fsdp")
    tokens, model = activations.shape
    rows, out_width = value_weight.shape
    rank = down_weight_pool.shape[1]
    steps = n // 4
    vmem = pl.BlockSpec(memory_space=pltpu.VMEM)
    hbm = pl.BlockSpec(memory_space=pl.ANY)
    smem = pl.BlockSpec(memory_space=pltpu.SMEM)
    dma = pltpu.SemaphoreType.DMA
    return pl.pallas_call(
        functools.partial(fused_kernel, n),
        out_shape=(
            jax.ShapeDtypeStruct((tokens, out_width), jnp.bfloat16),
            jax.ShapeDtypeStruct((tokens, model), jnp.bfloat16),
            jax.ShapeDtypeStruct((1, rank, model), jnp.float32),
            jax.ShapeDtypeStruct((1, rank, out_width), jnp.float32),
        ),
        in_specs=[hbm, vmem, vmem, smem, smem, hbm, vmem, vmem],
        out_specs=[vmem, hbm, vmem, vmem],
        scratch_shapes=[
            pltpu.VMEM((n, rows, out_width), jnp.bfloat16),
            pltpu.VMEM((tokens, out_width), jnp.bfloat16),
            pltpu.VMEM((tokens, out_width), jnp.float32),
            pltpu.VMEM((4, n, rank, model // n + LANES), jnp.bfloat16),
            pltpu.VMEM((n, rank, model // n + LANES), jnp.bfloat16),
            pltpu.VMEM((n, rank, model // n + LANES), jnp.bfloat16),
            pltpu.VMEM((n, rank, model // n + LANES), jnp.bfloat16),
            pltpu.VMEM((n, rank, model // n + LANES), jnp.bfloat16),
            pltpu.SMEM((n,), jnp.int32),
            pltpu.VMEM((tokens, rank), jnp.bfloat16),
            pltpu.VMEM((tokens, 1), jnp.float32),
            pltpu.VMEM((tokens, model), jnp.bfloat16),
            pltpu.VMEM((tokens, model), jnp.bfloat16),
            dma,
            dma((n,)),
            dma,
        ]
        + [dma((2, steps, 2))] * 2
        + [dma((2, steps))] * 2
        + [dma((2, steps, 2))] * 2
        + [dma((2, steps))] * 2
        + [dma, dma, dma((4, n)), dma((4, n))],
        compiler_params=pltpu.CompilerParams(
            collective_id=0, has_side_effects=True, vmem_limit_bytes=56 * 2**20
        ),
        cost_estimate=pl.CostEstimate(
            flops=4 * tokens * model * out_width,
            bytes_accessed=4 * tokens * model + 4 * model * out_width // n,
            transcendentals=0,
        ),
    )(
        activations,
        grad_out,
        token_tenant.reshape(1, tokens),
        segment_offsets,
        page_table,
        value_weight,
        down_weight_pool,
        up_weight_pool,
    )


def either(*args):
    n = lax.axis_size("fsdp")
    tokens, model = args[0].shape
    rows, out_width = args[4].shape
    slots, rank = args[5].shape[:2]
    fits = (
        lax.axis_size("groups") == 2
        and n % 8 == 0
        and n <= 32
        and tokens == BLOCK
        and slots == 1
        and rank % 16 == 0
        and model % (n * LANES) == 0
        and out_width % LANES == 0
        and out_width // LANES <= n
        and rows >= 128
        and rows % 16 == 0
    )
    return (fused if fits else on_device)(*args)


def solution(mesh):
    placed = (
        P(("groups", "fsdp"), None),
        P(("groups", "fsdp"), None),
        P(("groups", "fsdp")),
        P("groups"),
        P("fsdp", None),
        P("fsdp", None, None),
        P("fsdp", None, None),
        P(),
    )
    return jax.shard_map(
        either,
        mesh=mesh,
        in_specs=placed,
        out_specs=(
            P(("groups", "fsdp"), None),
            P(("groups", "fsdp"), None),
            P(("groups", "fsdp"), None, None),
            P(("groups", "fsdp"), None, None),
        ),
        check_vma=False,
    )
```
